512 devices in a mesh: guidance: 2 (over core), context: 16 (over z), head: 16 (over x, y).
Axes of the slice: x: 4, y: 4, z: 16, core: 2. Of those that a mesh axis runs over, the one named last changes fastest.
Arguments:
- tokens: bfloat16 [49152, 3072], P(('guidance', 'context', 'head')), parts along dimension 0, may hold values from -6 to 6
- w_query: bfloat16 [3072, 3072], P('context', 'head'), may hold values from -0.109375 to 0.109375
- w_key: bfloat16 [3072, 3072], P('context', 'head'), may hold values from -0.109375 to 0.109375
- w_value: bfloat16 [3072, 3072], P('context', 'head'), may hold values from -0.109375 to 0.109375
- w_out: bfloat16 [3072, 3072], P('context', 'head'), may hold values from -0.109375 to 0.109375
- q_gain: float32 [64], replicated, may hold values from 0.5 to 8
- k_gain: float32 [64], replicated, may hold values from 0.5 to 8
- key_tiles: int32 [384, 8], P('context'), may hold values from 0 to 383, as said below
- key_count: int32 [384], P('context'), may hold values from 3 to 8, as said below
Outputs:
- projected_out: bfloat16 [49152, 3072], P(('guidance', 'context'), 'head'), parts along dimension 0
The draws below stay inside these ranges and needn't reach their ends.
There are 2 independent parts, one for each index of `guidance`. The reference program is written for one: setup_inputs(seed, part) draws one part's arguments, and reference() takes and returns one part's arrays. A program takes and returns all parts, laid end to end along the dimension named above; an argument that names none is the same for every part. Nothing has to cross between parts.
Inputs may be any that keep to these rules, and one draw needn't show every extreme that they name: `key_tiles`: row q holds 8 different tiles, each in the frame of query tile q or one frame before or after, within one tile row and one tile column of it; the first is tile q itself. `key_count`: the first tile of every frame uses all 8.
All inputs are finite; a program needn't handle non-finite values.
Results may differ from the reference program's by a relative error of at most 0.0075.
The reference program's roundings to bfloat16 on the way (of `query`, `key`, `value`, `weights` and `attended`) count: a program that leaves them out, or rounds other values in their place, can miss the bound.
Values may be sent and summed in bfloat16 or wider, within the bound.
A program may use at most 64 MiB of HBM per device.

```python
import math
import jax
import jax.numpy as jnp
from jax import lax

D = 3072
HEADS = 48
HEAD_DIM = 64
INNER = 3072
FRAME_H = 30
FRAME_W = 45
TS = 8
TILES_H = 4
TILES_W = 6
TILES = 24
SLOTS = 1536
KT = 8
NF = 16


def gain_values(key, lower, upper):
    share = jax.random.uniform(key, (HEAD_DIM,), jnp.float32)
    return jnp.exp(jnp.log(lower) + share * (jnp.log(upper) - jnp.log(lower))).astype(jnp.float32)


def draw_q_gain(key, part):
    key = jax.random.fold_in(key, 13)
    return gain_values(key, 0.7, 2.0)


def draw_k_gain(key, part):
    key = jax.random.fold_in(key, 14)
    return gain_values(key, 0.7, 2.0)


def draw_key_tiles(key, part):
    key = jax.random.fold_in(key, 11)
    total = NF * TILES
    tile = jnp.arange(total, dtype=jnp.int32)
    frame = tile // TILES
    within = tile % TILES
    tile_row = within // TILES_W
    tile_col = within % TILES_W
    option = jnp.arange(27, dtype=jnp.int32)
    frame_step = option // 9 - 1
    row_step = option // 3 % 3 - 1
    col_step = option % 3 - 1
    near_frame = frame[:, None] + frame_step[None, :]
    near_row = tile_row[:, None] + row_step[None, :]
    near_col = tile_col[:, None] + col_step[None, :]
    valid = (near_frame >= 0) & (near_frame < NF) & (near_row >= 0) & (near_row < TILES_H)
    valid = valid & (near_col >= 0) & (near_col < TILES_W)
    prior = jnp.where(option == 13, 0, jnp.where((row_step == 0) & (col_step == 0), 1, 2))
    prior = jnp.where(valid, prior[None, :], 9)
    noise = jax.random.randint(key, (total, 27), 0, 1000)
    score = prior * 100000 + noise * 32 + option[None, :]
    order = jnp.argsort(score, axis=1)[:, :KT]
    ident = near_frame * TILES + near_row * TILES_W + near_col
    return jnp.take_along_axis(ident, order, axis=1).astype(jnp.int32)


def draw_key_count(key, part):
    key = jax.random.fold_in(key, 12)
    total = NF * TILES
    counts = jax.random.randint(key, (total,), 3, KT + 1)
    first = jnp.arange(total, dtype=jnp.int32) % TILES == 0
    return jnp.where(first, KT, counts).astype(jnp.int32)


def level_of(key, shape, split, smallest, top_value):
    def one(dim, blocks):
        heights = jax.random.uniform(jax.random.fold_in(jax.random.fold_in(key, 6), dim), (blocks,), jnp.float32, smallest / len(split), top_value / len(split))
        return jnp.repeat(jnp.exp(heights), shape[dim] // blocks).reshape((-1,) + (1,) * (len(shape) - dim - 1))

    factor_of = one(*split[0])
    for cut in split[1:]:
        factor_of = factor_of * one(*cut)
    return factor_of


def bell_draw(own_key, dims, scale, limit, split=(), kind=jnp.bfloat16):
    values = scale * jax.random.normal(own_key, dims, jnp.float32)
    if split:
        values = values * level_of(own_key, dims, split, -0.22, 0.18)
    return jnp.clip(values, -limit, limit).astype(kind)


def setup_inputs(seed: int = 0, part: int = 0) -> dict:
    arg_keys = jax.random.split(jax.random.key(seed), 10)
    part_keys = jax.random.split(jax.random.fold_in(arg_keys[9], part), 10)
    return {
        "tokens": bell_draw(part_keys[0], (NF * SLOTS, D), 1.0, 6.0, ((0, 256),)),
        "w_query": bell_draw(arg_keys[1], (D, INNER), D ** -0.5, 0.109375, ((0, 16), (1, 16))),
        "w_key": bell_draw(arg_keys[2], (D, INNER), D ** -0.5, 0.109375, ((0, 16), (1, 16))),
        "w_value": bell_draw(arg_keys[3], (D, INNER), D ** -0.5, 0.109375, ((0, 16), (1, 16))),
        "w_out": bell_draw(arg_keys[4], (INNER, D), INNER ** -0.5, 0.109375, ((0, 16), (1, 16))),
        "q_gain": draw_q_gain(jax.random.fold_in(arg_keys[9], 71), part),
        "k_gain": draw_k_gain(jax.random.fold_in(arg_keys[9], 71), part),
        "key_tiles": draw_key_tiles(jax.random.fold_in(arg_keys[9], 71), part),
        "key_count": draw_key_count(jax.random.fold_in(arg_keys[9], 71), part),
    }


def layer_norm(values, gain):
    mean = lax.optimization_barrier(jnp.mean(values, axis=-1, keepdims=True))
    centred = values - mean
    spread = lax.optimization_barrier(jnp.mean(centred * centred, axis=-1, keepdims=True))
    return centred * lax.rsqrt(spread + 1e-06) * gain

def slot_live(tile_ids):
    within = tile_ids % TILES
    slots = jnp.arange(TS * TS, dtype=jnp.int32)
    grid_row = (within // TILES_W)[..., None] * TS + slots // TS
    grid_col = (within % TILES_W)[..., None] * TS + slots % TS
    return (grid_row < FRAME_H) & (grid_col < FRAME_W)

def attend(queries, keys, values, keep):
    scale = 1.0 / math.sqrt(HEAD_DIM)
    scores = jnp.einsum('tqhe,tkhe->thqk', queries.astype(jnp.float32), keys.astype(jnp.float32)) * scale
    mask = keep[:, None, None, :]
    scores = jnp.where(mask, scores, -jnp.inf)
    top = lax.optimization_barrier(jnp.max(scores, axis=-1, keepdims=True))
    expo = jnp.where(mask, jnp.exp(scores - top), 0.0)
    weights = (expo / lax.optimization_barrier(jnp.sum(expo, axis=-1, keepdims=True))).astype(jnp.bfloat16)
    return jnp.einsum('thqk,tkhe->tqhe', weights.astype(jnp.float32), values.astype(jnp.float32))

def reference(tokens, w_query, w_key, w_value, w_out, q_gain, k_gain, key_tiles, key_count):
    area = TS * TS
    total_tiles = NF * TILES

    def project(weight):
        raw = jnp.dot(tokens, weight, preferred_element_type=jnp.float32)
        return raw.reshape(total_tiles, area, HEADS, HEAD_DIM)
    query = layer_norm(project(w_query), q_gain).astype(jnp.bfloat16)
    key = layer_norm(project(w_key), k_gain).astype(jnp.bfloat16)
    value = project(w_value).astype(jnp.bfloat16)
    in_use = jnp.arange(KT, dtype=jnp.int32)[None, :] < key_count[:, None]

    def one_frame(frame):
        start = (frame * TILES).astype(jnp.int32)
        lists = lax.dynamic_slice_in_dim(key_tiles, start, TILES, 0)
        used = lax.dynamic_slice_in_dim(in_use, start, TILES, 0)
        queries = lax.dynamic_slice_in_dim(query, start, TILES, 0)
        keys = key[lists].reshape(TILES, KT * area, HEADS, HEAD_DIM)
        values = value[lists].reshape(TILES, KT * area, HEADS, HEAD_DIM)
        keep = (used[:, :, None] & slot_live(lists)).reshape(TILES, KT * area)
        result = attend(queries, keys, values, keep)
        own = slot_live(jnp.arange(TILES, dtype=jnp.int32))
        attended = jnp.where(own[:, :, None, None], result, 0.0).astype(jnp.bfloat16)
        flat = attended.reshape(SLOTS, INNER)
        return jnp.dot(flat, w_out, preferred_element_type=jnp.float32).astype(jnp.bfloat16)
    frames = lax.map(one_frame, jnp.arange(NF, dtype=jnp.int32))
    return frames.reshape(NF * SLOTS, D)
```

```python
import functools

import jax
import jax.numpy as jnp
from jax import lax
from jax.experimental import pallas as pl
from jax.experimental.pallas import tpu as pltpu
from jax.sharding import PartitionSpec as P

HEAD_DIM = 64
FRAME_H = 30
FRAME_W = 45
TILES_W = 6
TILES = 24
SLOTS = 1536
KT = 8
SIDE = 4
DEPTH = 16
D = 3072
MESH = pl.DeviceIdType.MESH
BF = jnp.bfloat16
F32 = jnp.float32


def place():
    g = lax.axis_index("guidance")
    z = lax.axis_index("context")
    h = lax.axis_index("head")
    return g, z, lax.div(h, SIDE), lax.rem(h, SIDE)


def at_xy(dx, dy):
    g, z, x, y = place()
    return (g, z, lax.rem(x + dx + SIDE, SIDE) * SIDE + lax.rem(y + dy + SIDE, SIDE))


def at_z(dz):
    g, z, x, y = place()
    return (g, lax.rem(z + dz + DEPTH, DEPTH), x * SIDE + y)


def sibling():
    g, z, x, y = place()
    return (1 - g, z, x * SIDE + y)


def send(src, dst, ssem, rsem, device):
    pltpu.make_async_remote_copy(
        src_ref=src, dst_ref=dst, send_sem=ssem, recv_sem=rsem, device_id=device, device_id_type=MESH
    ).start()


def wait_recv(dst, ssem, rsem):
    pltpu.make_async_remote_copy(
        src_ref=dst, dst_ref=dst, send_sem=ssem, recv_sem=rsem, device_id=sibling(), device_id_type=MESH
    ).wait_recv()


def wait_send(src, ssem, rsem):
    pltpu.make_async_remote_copy(
        src_ref=src, dst_ref=src, send_sem=ssem, recv_sem=rsem, device_id=sibling(), device_id_type=MESH
    ).wait_send()


def greet(partners):
    barrier = pltpu.get_barrier_semaphore()
    for partner in partners:
        pl.semaphore_signal(barrier, inc=1, device_id=partner, device_id_type=MESH)
    pl.semaphore_wait(barrier, len(partners))


def head_norm(raw, gain):
    lane_a = lax.broadcasted_iota(jnp.int32, (256, 256), 0) // HEAD_DIM
    lane_b = lax.broadcasted_iota(jnp.int32, (256, 256), 1) // HEAD_DIM
    pick = jnp.where(lane_a == lane_b, 1.0 / HEAD_DIM, 0.0).astype(BF)

    def mean(values):
        high = values.astype(BF)
        low = (values - high.astype(F32)).astype(BF)
        return jnp.dot(high, pick, preferred_element_type=F32) + jnp.dot(
            low, pick, preferred_element_type=F32
        )

    centred = raw - mean(raw)
    spread = mean(centred * centred)
    return centred * lax.rsqrt(spread + 1e-06) * gain


HALF = 48
COLS = D // 2


def project_kernel(
    tok_ref, wq_ref, wk_ref, wv_ref, wo_ref, qg_ref, kg_ref,
    q_ref, kv_ref, woq_ref,
    toks, wvk, tsend, trecv, zsend, zrecv, ssend, srecv, hsend, hrecv,
):
    g, z, x, y = place()
    greet([at_xy(1, 0), at_xy(-1, 0), at_xy(0, 1), at_xy(0, -1), at_z(1), at_z(-1), sibling()])
    sent = []

    def ship(src, dst, ssem, rsem, device):
        send(src, dst, ssem, rsem, device)
        sent.append((src, ssem, rsem))

    def axis_dev(p, second, step):
        along_x = (p == 0) != second
        return at_xy(step, 0) if along_x else at_xy(0, step)

    def cols(d):
        return pl.ds(d * COLS, COLS)

    def piece(p, ra, rb, d):
        return toks.at[p, ra, rb, :, cols(d)]

    def own(p, d):
        return tok_ref.at[pl.ds(p * HALF, HALF), cols(d)]

    def ship_first(p):
        for k, (d, step) in enumerate(((0, 1), (1, -1), (1, 1), (0, -1))):
            ra = 3 if step == 1 else 1
            ship(own(p, d), piece(p, ra, 0, d), tsend.at[p, 4, k], trecv.at[p, ra, 0, d], axis_dev(p, False, step))

    def ship_second(p, ra):
        for k, (d, step) in enumerate(((0, 1), (1, -1), (1, 1), (0, -1))):
            rb = 3 if step == 1 else 1
            src = own(p, d) if ra == 0 else piece(p, ra, 0, d)
            ship(src, piece(p, ra, rb, d), tsend.at[p, ra, k], trecv.at[p, ra, rb, d], axis_dev(p, True, step))

    def got(p, ra, rb, d):
        wait_recv(piece(p, ra, rb, d), tsend.at[p, 0, 0], trecv.at[p, ra, rb, d])

    def relay_first(p):
        got(p, 3, 0, 0)
        ship(piece(p, 3, 0, 0), piece(p, 2, 0, 0), tsend.at[p, 4, 4], trecv.at[p, 2, 0, 0], axis_dev(p, False, 1))
        got(p, 1, 0, 1)
        ship(piece(p, 1, 0, 1), piece(p, 2, 0, 1), tsend.at[p, 4, 5], trecv.at[p, 2, 0, 1], axis_dev(p, False, -1))

    def relay_second(p, ra):
        got(p, ra, 3, 0)
        ship(piece(p, ra, 3, 0), piece(p, ra, 2, 0), tsend.at[p, ra, 4], trecv.at[p, ra, 2, 0], axis_dev(p, True, 1))
        got(p, ra, 1, 1)
        ship(piece(p, ra, 1, 1), piece(p, ra, 2, 1), tsend.at[p, ra, 5], trecv.at[p, ra, 2, 1], axis_dev(p, True, -1))

    def rest_second(p, ra):
        got(p, ra, 3, 1)
        got(p, ra, 1, 0)
        got(p, ra, 2, 0)
        got(p, ra, 2, 1)

    def block(part, dz):
        ref = wvk if part == 0 else woq_ref
        return ref.at[lax.rem(z + dz + DEPTH, DEPTH), pl.ds(pl.multiple_of(g * 96, 96), 96), :]

    def other_block(part, dz):
        ref = wvk if part == 0 else woq_ref
        return ref.at[lax.rem(z + dz + DEPTH, DEPTH), pl.ds(pl.multiple_of((1 - g) * 96, 96), 96), :]

    def steps(part, way):
        return 8 if (part == 0) == (way == 0) else 7

    def ship_weights(part, way, s):
        dz = -s if way == 0 else s
        ship(block(part, dz), block(part, dz), zsend.at[part, way, s], zrecv.at[part, way, s], at_z(1 if way == 0 else -1))

    def weight_step(part, way, s):
        dz = -s if way == 0 else s
        if s > steps(part, way):
            return
        wait_recv(block(part, dz), zsend.at[part, way, 0], zrecv.at[part, way, s - 1])
        if s < steps(part, way):
            ship_weights(part, way, s)
        ship(block(part, dz), block(part, dz), ssend.at[part, way, s - 1], srecv.at[part, way, s - 1], sibling())

    def weight_round(s):
        for part in range(2):
            for way in range(2):
                weight_step(part, way, s)

    def weights_shared(part):
        for way in range(2):
            for s in range(1, steps(part, way) + 1):
                dz = -s if way == 0 else s
                wait_recv(other_block(part, dz), ssend.at[part, way, 0], srecv.at[part, way, s - 1])

    wvk[z] = jnp.concatenate([wv_ref[...], wk_ref[...]], axis=1)
    woq_ref[z] = jnp.concatenate([wo_ref[...], wq_ref[...]], axis=1)
    for part in range(2):
        for way in range(2):
            ship_weights(part, way, 0)
        if part == 0:
            ship_first(0)
            ship_first(1)
    for p in range(2):
        toks[p, 0, 0] = tok_ref[pl.ds(p * HALF, HALF), :]

    lane = lax.broadcasted_iota(jnp.int32, (1, 256), 1)
    q_gain = jnp.concatenate([qg_ref[...]] * 4, axis=1) * 0.125
    k_gain = jnp.concatenate([kg_ref[...]] * 4, axis=1)

    def rows_of(p, ra, rb):
        da, db = (x, y) if not isinstance(p, int) or p == 0 else (y, x)
        if not isinstance(p, int):
            a_x = jnp.where(p == 0, ra, rb)
            a_y = jnp.where(p == 0, rb, ra)
        else:
            a_x, a_y = (ra, rb) if p == 0 else (rb, ra)
        xs = lax.rem(x + a_x, SIDE)
        ys = lax.rem(y + a_y, SIDE)
        return pl.multiple_of(xs * 384 + ys * 96 + p * HALF, 16)

    def group(ra):
        def one(p, carry):
            rows = toks[p, ra].reshape(4 * HALF, D)
            raw_v = jnp.dot(rows, wvk[:, :, 0:128].reshape(D, 128), preferred_element_type=F32)
            raw_k = jnp.dot(rows, wvk[:, :, 128:384].reshape(D, 256), preferred_element_type=F32)
            raw_q = jnp.dot(rows, woq_ref[:, :, 128:384].reshape(D, 256), preferred_element_type=F32)
            key = jnp.where(lane >= HEAD_DIM, head_norm(raw_k, k_gain), raw_k)
            query = jnp.where(lane >= HEAD_DIM, head_norm(raw_q, q_gain), 0.0).astype(BF)
            keyval = jnp.concatenate([raw_v, key], axis=1).astype(BF)
            for rb in range(4):
                at = rows_of(p, ra, rb)
                q_ref[pl.ds(at, HALF), :] = query[rb * HALF : (rb + 1) * HALF]
                kv_ref[1, pl.ds(at, HALF), :] = keyval[rb * HALF : (rb + 1) * HALF]
            return carry

        lax.fori_loop(0, 2, one, 0)
        for p in range(2):
            for rb in range(4):
                here = pl.ds(rows_of(p, ra, rb), HALF)
                for way in range(2):
                    ship(
                        kv_ref.at[1, here, :], kv_ref.at[2 * way, here, :],
                        hsend.at[p, ra, rb, way], hrecv.at[p, ra, rb, way], at_z(1 - 2 * way),
                    )

    weight_round(1)
    for p in range(2):
        relay_first(p)
    for p in range(2):
        ship_second(p, 0)
    weight_round(2)
    weight_round(3)
    for p in range(2):
        got(p, 3, 0, 1)
        got(p, 1, 0, 0)
        ship_second(p, 3)
    weight_round(4)
    for p in range(2):
        relay_second(p, 0)
    weight_round(5)
    for p in range(2):
        ship_second(p, 1)
    weight_round(6)
    for p in range(2):
        got(p, 2, 0, 0)
        got(p, 2, 0, 1)
    for p in range(2):
        relay_second(p, 3)
    weight_round(7)
    for p in range(2):
        ship_second(p, 2)
    weight_round(8)
    for p in range(2):
        rest_second(p, 0)
    weights_shared(0)
    weights_shared(1)
    group(0)
    for p in range(2):
        relay_second(p, 1)
        rest_second(p, 3)
    group(3)
    for p in range(2):
        relay_second(p, 2)
        rest_second(p, 1)
    group(1)
    for p in range(2):
        rest_second(p, 2)
    group(2)
    for src, ssem, rsem in sent:
        wait_send(src, ssem, rsem)
    for ra in range(4):
        for p in range(2):
            for rb in range(4):
                here = pl.ds(rows_of(p, ra, rb), HALF)
                for way in range(2):
                    wait_recv(kv_ref.at[2 * way, here, :], hsend.at[0, 0, 0, 0], hrecv.at[p, ra, rb, way])


def project(tokens, w_query, w_key, w_value, w_out, q_gain, k_gain):
    vmem = pl.BlockSpec(memory_space=pltpu.VMEM)
    sems = pltpu.SemaphoreType.DMA
    return pl.pallas_call(
        project_kernel,
        out_shape=(
            jax.ShapeDtypeStruct((SLOTS, 256), BF),
            jax.ShapeDtypeStruct((3, SLOTS, 384), BF),
            jax.ShapeDtypeStruct((DEPTH, 192, 384), BF),
        ),
        in_specs=[vmem] * 7,
        out_specs=(vmem,) * 3,
        scratch_shapes=[
            pltpu.VMEM((2, 4, 4, HALF, D), BF),
            pltpu.VMEM((DEPTH, 192, 384), BF),
            sems((2, 5, 6)), sems((2, 4, 4, 2)),
            sems((2, 2, 8)), sems((2, 2, 8)),
            sems((2, 2, 8)), sems((2, 2, 8)),
            sems((2, 4, 4, 2)), sems((2, 4, 4, 2)),
        ],
        compiler_params=pltpu.CompilerParams(
            collective_id=0, has_side_effects=True, vmem_limit_bytes=56 * 1024 * 1024
        ),
        name="project",
    )(tokens, w_query, w_key, w_value, w_out, q_gain[None, :], k_gain[None, :])


def attend_kernel(
    tiles_ref, count_ref, q_ref, kv_ref, woq_ref,
    out_ref,
    wos, att, gat, acc, outs, wsend, wrecv, vsend, vrecv, asend, arecv, ysend, yrecv, osend, orecv,
):
    g, z, x, y = place()
    greet([at_xy(1, 0), at_xy(-1, 0), at_xy(2, 0), at_xy(0, 1), at_xy(0, -1), sibling()])
    sent = []

    def ship(src, dst, ssem, rsem, device):
        send(src, dst, ssem, rsem, device)
        sent.append((src, ssem, rsem))

    def wout(ra, c, half):
        return wos.at[ra, pl.ds(c * 8, 8), pl.ds(pl.multiple_of(64 + half * 96, 32), 96), :]

    for c in range(2):
        for k, (step, ra) in enumerate(((1, 3), (-1, 1))):
            ship(
                woq_ref.at[pl.ds(c * 8, 8), pl.ds(pl.multiple_of(g * 96, 96), 96), pl.ds(0, 256)],
                wout(ra, c, g), wsend.at[ra, c], wrecv.at[ra, c], at_xy(step, 0),
            )

    def wout_got(ra, c):
        wait_recv(wout(ra, c, g), wsend.at[0, 0], wrecv.at[ra, c])
        if ra == 3 and c == 0:
            ship(wout(3, 0, g), wout(2, 0, g), wsend.at[2, 0], wrecv.at[2, 0], at_xy(1, 0))
        if ra == 1 and c == 1:
            ship(wout(1, 1, g), wout(2, 1, g), wsend.at[2, 1], wrecv.at[2, 1], at_xy(-1, 0))
        ship(wout(ra, c, g), wout(ra, c, g), vsend.at[ra, c], vrecv.at[ra, c], sibling())

    wos[:, :, 0:64, :] = jnp.zeros((4, DEPTH, 64, 256), BF)
    wos[0, :, 64:256, :] = woq_ref[:, :, 0:256]
    acc[...] = jnp.zeros_like(acc)

    lane = lax.broadcasted_iota(jnp.int32, (1, 256), 1)
    key_lane = lax.broadcasted_iota(jnp.int32, (1, KT * 64), 1)
    slot = lax.rem(key_lane, 64)
    rank = lax.div(key_lane, 64)
    low_row = lax.div(slot, 8) < FRAME_H - 24
    low_col = lax.rem(slot, 8) < FRAME_W - 40
    row_slot = lax.broadcasted_iota(jnp.int32, (64, 1), 0)

    def attend_tile(tile):
        queries = q_ref[pl.ds(pl.multiple_of(tile * 64, 64), 64), :]
        stacked = jnp.concatenate(
            [jnp.where(lax.div(lane, 64) == h + 1, queries, jnp.zeros_like(queries)) for h in range(3)], axis=0
        )
        count = count_ref[tile]
        near = []
        row_last = jnp.zeros_like(key_lane)
        col_last = jnp.zeros_like(key_lane)
        for j in range(KT):
            index = jnp.clip(tiles_ref[tile, j] - (z - 1) * TILES, 0, 3 * TILES - 1)
            near.append(kv_ref[index])
            within = lax.rem(index, TILES)
            here = rank == j
            row_last = jnp.where(here, (within >= 18).astype(jnp.int32), row_last)
            col_last = jnp.where(here, (lax.rem(within, TILES_W) == TILES_W - 1).astype(jnp.int32), col_last)
        near = jnp.concatenate(near, axis=0)
        keep = (rank < count) & ((row_last == 0) | low_row) & ((col_last == 0) | low_col)
        scores = lax.dot_general(
            stacked, near[:, 128:384], (((1,), (1,)), ((), ())), preferred_element_type=F32
        )
        scores = jnp.where(keep, scores, -1e30)
        top = jnp.max(scores, axis=-1, keepdims=True)
        weights = jnp.exp(scores - top).astype(BF)
        values = jnp.where(lane >= 192, jnp.ones((), BF), near[:, 0:256])
        mixed = jnp.dot(weights, values, preferred_element_type=F32)
        mixed = mixed / mixed[:, 192:193]
        result = jnp.where(
            lane < 64, mixed[0:64], jnp.where(lane < 128, mixed[64:128], mixed[128:192])
        )
        row, col = lax.div(tile, TILES_W), lax.rem(tile, TILES_W)
        alive = (row * 8 + lax.div(row_slot, 8) < FRAME_H) & (col * 8 + lax.rem(row_slot, 8) < FRAME_W)
        return jnp.where(alive, result, 0.0)

    def attend_row(k, row):
        def one(i, carry):
            left = attend_tile(row * TILES_W + i)
            right = pltpu.roll(attend_tile(row * TILES_W + 3 + i), 64, 1)
            middle = jnp.where(lane[:, 0:128] < 64, left[:, 128:256], right[:, 0:128])
            packed = jnp.concatenate([left[:, 0:128], middle, right[:, 128:256]], axis=1).astype(BF)
            att[k, pl.ds(pl.multiple_of(i * 64, 64), 64), :] = packed
            return carry

        lax.fori_loop(0, 3, one, 0)

    def piece(ra, rb, d):
        return gat.at[ra, rb, pl.ds(d * 96, 96), :]

    def ship_y(ra):
        for k, (d, step) in enumerate(((0, 1), (1, -1), (1, 1), (0, -1))):
            rb = 3 if step == 1 else 1
            src = att.at[0, pl.ds(d * 96, 96), :] if ra == 0 else piece(ra, 0, d)
            ship(src, piece(ra, rb, d), ysend.at[ra, k], yrecv.at[ra, rb, d], at_xy(0, step))

    def got_y(ra, rb, d):
        wait_recv(piece(ra, rb, d), ysend.at[0, 0], yrecv.at[ra, rb, d])

    def relay_y(ra):
        got_y(ra, 3, 0)
        ship(piece(ra, 3, 0), piece(ra, 2, 0), ysend.at[ra, 4], yrecv.at[ra, 2, 0], at_xy(0, 1))
        got_y(ra, 1, 1)
        ship(piece(ra, 1, 1), piece(ra, 2, 1), ysend.at[ra, 5], yrecv.at[ra, 2, 1], at_xy(0, -1))

    def rest_y(ra):
        got_y(ra, 3, 1)
        got_y(ra, 1, 0)
        got_y(ra, 2, 0)
        got_y(ra, 2, 1)

    def add_source(ra, rb, own=False):
        h = lax.rem(x + ra, SIDE) * SIDE + lax.rem(y + rb, SIDE)
        rows = att[0] if own else gat[ra, rb]
        for xi in range(4):
            acc[xi, 0:192, :] += jnp.dot(rows[:, 0:192], wos[xi, h, 64:256, :], preferred_element_type=F32)
            acc[xi, 192:384, :] += jnp.dot(rows[:, 128:384], wos[xi, h, :, :], preferred_element_type=F32)

    def ship_x(k):
        ship(att.at[k], gat.at[4 - k, 0], asend.at[k], arecv.at[4 - k], at_xy(k, 0))

    def got_x(ra):
        wait_recv(gat.at[ra, 0], asend.at[0], arecv.at[ra])

    attend_row(0, x)
    ship_y(0)
    attend_row(1, lax.rem(x + 1, SIDE))
    ship_x(1)
    wout_got(3, 0)
    wout_got(1, 1)
    attend_row(3, lax.rem(x + 3, SIDE))
    ship_x(3)
    wout_got(3, 1)
    wout_got(1, 0)
    relay_y(0)
    attend_row(2, lax.rem(x + 2, SIDE))
    ship_x(2)
    got_x(3)
    ship_y(3)
    got_x(1)
    ship_y(1)
    rest_y(0)
    relay_y(3)
    got_x(2)
    ship_y(2)
    wout_got(2, 0)
    wout_got(2, 1)
    for ra in range(1, 4):
        for c in range(2):
            wait_recv(wout(ra, c, 1 - g), vsend.at[0, 0], vrecv.at[ra, c])
    add_source(0, 0, True)
    relay_y(1)

    def add_row(ra, first):
        def one(rb, carry):
            add_source(ra, rb)
            return carry

        lax.fori_loop(first, 4, one, 0)

    add_row(0, 1)
    rest_y(3)
    relay_y(2)
    add_row(3, 0)
    rest_y(1)
    add_row(1, 0)
    rest_y(2)
    add_row(2, 0)
    for xi in (2, 1, 3, 0):
        if xi == 0:
            outs[0] = acc[0].astype(BF)
        else:
            att_out = acc[xi].astype(BF)
            outs[4 + xi] = att_out
            ship(outs.at[4 + xi], outs.at[4 - xi], osend.at[xi], orecv.at[4 - xi], at_xy(xi, 0))
    for ra in (0, 3, 1, 2):
        if ra:
            wait_recv(outs.at[ra], osend.at[0], orecv.at[ra])
        at = pl.multiple_of(lax.rem(x + ra, SIDE) * 384, 384)
        out_ref[pl.ds(at, 384), :] = outs[ra][:, 0:192]
    for src, ssem, rsem in sent:
        wait_send(src, ssem, rsem)


def attend_and_project(key_tiles, key_count, query, keyval, woq):
    vmem = pl.BlockSpec(memory_space=pltpu.VMEM)
    smem = pl.BlockSpec(memory_space=pltpu.SMEM)
    sems = pltpu.SemaphoreType.DMA
    return pl.pallas_call(
        attend_kernel,
        out_shape=jax.ShapeDtypeStruct((SLOTS, 192), BF),
        in_specs=[smem, smem, vmem, vmem, vmem],
        out_specs=vmem,
        scratch_shapes=[
            pltpu.VMEM((4, DEPTH, 256, 256), BF),
            pltpu.VMEM((4, 192, 384), BF),
            pltpu.VMEM((4, 4, 192, 384), BF),
            pltpu.VMEM((4, 384, 256), F32),
            pltpu.VMEM((8, 384, 256), BF),
            sems((4, 2)), sems((4, 2)),
            sems((4, 2)), sems((4, 2)),
            sems((4,)), sems((4,)),
            sems((4, 6)), sems((4, 4, 2)),
            sems((4,)), sems((4,)),
        ],
        compiler_params=pltpu.CompilerParams(
            collective_id=1, has_side_effects=True, vmem_limit_bytes=56 * 1024 * 1024
        ),
        name="attend",
    )(key_tiles, key_count, query, keyval, woq)


def on_device(tokens, w_query, w_key, w_value, w_out, q_gain, k_gain, key_tiles, key_count):
    query, keyval, woq = project(tokens, w_query, w_key, w_value, w_out, q_gain, k_gain)
    return attend_and_project(key_tiles, key_count, query, keyval.reshape(3 * TILES, 64, 384), woq)


def solution(mesh):
    in_specs = (
        P(("guidance", "context", "head"), None),
        P("context", "head"),
        P("context", "head"),
        P("context", "head"),
        P("context", "head"),
        P(),
        P(),
        P("context", None),
        P("context"),
    )
    out_specs = P(("guidance", "context"), "head")
    return jax.shard_map(
        on_device, mesh=mesh, in_specs=in_specs, out_specs=out_specs, check_vma=False
    )
```

```python
import jax
import jax.numpy as jnp
from jax import lax
from jax.experimental import pallas as pl
from jax.experimental.pallas import tpu as pltpu
from jax.sharding import PartitionSpec as P

HEAD_DIM = 64
FRAME_H = 30
FRAME_W = 45
TILES_W = 6
TILES = 24
SLOTS = 1536
KT = 8
SIDE = 4
DEPTH = 16
D = 3072
MESH = pl.DeviceIdType.MESH
BF = jnp.bfloat16
F32 = jnp.float32


def place():
    g = lax.axis_index("guidance")
    z = lax.axis_index("context")
    h = lax.axis_index("head")
    return g, z, lax.div(h, SIDE), lax.rem(h, SIDE)


def at_xy(dx, dy):
    g, z, x, y = place()
    return (g, z, lax.rem(x + dx + SIDE, SIDE) * SIDE + lax.rem(y + dy + SIDE, SIDE))


def at_z(dz):
    g, z, x, y = place()
    return (g, lax.rem(z + dz + DEPTH, DEPTH), x * SIDE + y)


def sibling():
    g, z, x, y = place()
    return (1 - g, z, x * SIDE + y)


def send(src, dst, ssem, rsem, device):
    pltpu.make_async_remote_copy(
        src_ref=src, dst_ref=dst, send_sem=ssem, recv_sem=rsem, device_id=device, device_id_type=MESH
    ).start()


def wait_recv(dst, ssem, rsem):
    pltpu.make_async_remote_copy(
        src_ref=dst, dst_ref=dst, send_sem=ssem, recv_sem=rsem, device_id=sibling(), device_id_type=MESH
    ).wait_recv()


def wait_send(src, ssem, rsem):
    pltpu.make_async_remote_copy(
        src_ref=src, dst_ref=src, send_sem=ssem, recv_sem=rsem, device_id=sibling(), device_id_type=MESH
    ).wait_send()


def greet(partners):
    barrier = pltpu.get_barrier_semaphore()
    for partner in partners:
        pl.semaphore_signal(barrier, inc=1, device_id=partner, device_id_type=MESH)
    pl.semaphore_wait(barrier, len(partners))


def head_norm(raw, gain):
    lane_a = lax.broadcasted_iota(jnp.int32, (256, 256), 0) // HEAD_DIM
    lane_b = lax.broadcasted_iota(jnp.int32, (256, 256), 1) // HEAD_DIM
    pick = jnp.where(lane_a == lane_b, 1.0 / HEAD_DIM, 0.0).astype(BF)

    def mean(values):
        high = values.astype(BF)
        low = (values - high.astype(F32)).astype(BF)
        return jnp.dot(high, pick, preferred_element_type=F32) + jnp.dot(
            low, pick, preferred_element_type=F32
        )

    centred = raw - mean(raw)
    spread = mean(centred * centred)
    return centred * lax.rsqrt(spread + 1e-06) * gain


HALF = 48
COLS = D // 2
WAYS = ((0, 1), (1, -1))
PARTS = ((0, 0, 48, 8), (0, 48, 48, 8), (1, 0, 96, 7), (2, 0, 96, 8))


def block_kernel(
    tiles_hbm, count_hbm, tok_ref, wq_ref, wk_ref, wv_ref, wo_ref, qg_ref, kg_ref,
    out_ref,
    tiles_ref, count_ref, toks, wvk, woq, query_ref, kv, wos, att, gat, acc, outs,
    csem, tsend, trecv, zsend, zrecv, ssend, srecv, hsend, hrecv,
    wsend, wrecv, vsend, vrecv, asend, arecv, ysend, yrecv, osend, orecv,
):
    g, z, x, y = place()
    lists = pltpu.make_async_copy(tiles_hbm, tiles_ref, csem.at[0])
    counts = pltpu.make_async_copy(count_hbm, count_ref, csem.at[1])
    lists.start()
    counts.start()
    greet([
        at_xy(1, 0), at_xy(-1, 0), at_xy(2, 0), at_xy(0, 1), at_xy(0, -1), at_z(1), at_z(-1), sibling()
    ])
    sent = []

    def ship(src, dst, ssem, rsem, device):
        send(src, dst, ssem, rsem, device)
        sent.append((src, ssem, rsem))

    def drain():
        for src, ssem, rsem in sent:
            wait_send(src, ssem, rsem)
        sent.clear()

    def axis_dev(p, second, step):
        along_x = (p == 0) != second
        return at_xy(step, 0) if along_x else at_xy(0, step)

    def piece(p, ra, rb, d):
        return toks.at[ra, p, rb, :, pl.ds(d * COLS, COLS)]

    def landing(p, rnd, rel, d):
        return piece(p, rel, 0, d) if rnd == 4 else piece(p, rnd, rel, d)

    def own(p, d):
        return tok_ref.at[pl.ds(p * HALF, HALF), pl.ds(d * COLS, COLS)]

    def arrival(p, rnd, rel, d):
        return trecv.at[p, rel, 0, d] if rnd == 4 else trecv.at[p, rnd, rel, d]

    def start(rnd, k):
        for p in range(2):
            for i, (d, step) in enumerate(WAYS):
                d = d ^ k
                src = own(p, d) if rnd in (0, 4) else piece(p, rnd, 0, d)
                rel = 3 if step == 1 else 1
                ship(src, landing(p, rnd, rel, d), tsend.at[p, rnd, 2 * k + i], arrival(p, rnd, rel, d),
                     axis_dev(p, rnd != 4, step))

    def got(p, rnd, rel, d):
        wait_recv(landing(p, rnd, rel, d), tsend.at[p, 0, 0], arrival(p, rnd, rel, d))

    def relay(rnd):
        for p in range(2):
            for i, (d, step) in enumerate(WAYS):
                rel = 3 if step == 1 else 1
                got(p, rnd, rel, d)
                ship(landing(p, rnd, rel, d), landing(p, rnd, 2, d), tsend.at[p, rnd, 4 + i],
                     arrival(p, rnd, 2, d), axis_dev(p, rnd != 4, step))

    def near_rest(rnd):
        for p in range(2):
            got(p, rnd, 3, 1)
            got(p, rnd, 1, 0)

    def far(rnd):
        for p in range(2):
            got(p, rnd, 2, 0)
            got(p, rnd, 2, 1)

    def block(part, dz, half):
        which, first, height, _ = PARTS[part]
        at = lax.rem(z + dz + DEPTH, DEPTH)
        rows = pl.ds(pl.multiple_of(half * 96 + first, 16), height)
        if which == 0:
            return wvk.at[at, rows, :]
        if which == 1:
            return woq.at[at, rows, :]
        return wos.at[0, at, pl.ds(pl.multiple_of(64 + half * 96, 32), height), pl.ds(0, 128)]

    def steps(part, way):
        count = PARTS[part][3]
        return count if way == 0 else 15 - count

    def ship_weights(part, way, s):
        dz = -s if way == 0 else s
        ship(block(part, dz, g), block(part, dz, g), zsend.at[part, way, s], zrecv.at[part, way, s],
             at_z(1 if way == 0 else -1))

    def weight_round(s, parts):
        for part in parts:
            for way in range(2):
                if s > steps(part, way):
                    continue
                dz = -s if way == 0 else s
                here = block(part, dz, g)
                wait_recv(here, zsend.at[part, way, 0], zrecv.at[part, way, s - 1])
                if s < steps(part, way):
                    ship_weights(part, way, s)
                ship(here, here, ssend.at[part, way, s - 1], srecv.at[part, way, s - 1], sibling())

    def weights_shared(parts):
        for part in parts:
            for way in range(2):
                for s in range(1, steps(part, way) + 1):
                    dz = -s if way == 0 else s
                    wait_recv(block(part, dz, 1 - g), ssend.at[part, way, 0], srecv.at[part, way, s - 1])

    start(4, 0)
    wvk[z] = jnp.concatenate([wv_ref[...], wk_ref[...]], axis=1)
    for part in (0, 1):
        for way in range(2):
            ship_weights(part, way, 0)
    start(4, 1)
    both = jnp.concatenate([wo_ref[...], wq_ref[...]], axis=1)
    woq[z] = both[:, 128:384]
    wos[0, z, 64:256, 0:128] = both[:, 0:128]
    for part in (2, 3):
        for way in range(2):
            ship_weights(part, way, 0)
    start(0, 0)
    for p in range(2):
        toks[0, p, 0] = tok_ref[pl.ds(p * HALF, HALF), :]
    wos[:, :, 0:64, :] = jnp.zeros((4, DEPTH, 64, 256), BF)
    acc[...] = jnp.zeros_like(acc)

    lane = lax.broadcasted_iota(jnp.int32, (1, 256), 1)
    q_gain = jnp.concatenate([qg_ref[...]] * 4, axis=1) * 0.125
    k_gain = jnp.concatenate([kg_ref[...]] * 4, axis=1)

    def unit(p, ra, rb):
        a_x, a_y = (ra, rb) if p == 0 else (rb, ra)
        return lax.rem(x + a_x, SIDE) * 24 + lax.rem(y + a_y, SIDE) * 6 + p * 3

    def group(ra):
        rows = toks[ra].reshape(8 * HALF, D)
        raw = jnp.dot(rows, wvk[...].reshape(D, 384), preferred_element_type=F32)
        raw_q = jnp.dot(rows, woq[...].reshape(D, 256), preferred_element_type=F32)
        raw_k = raw[:, 128:384]
        key = jnp.where(lane >= HEAD_DIM, head_norm(raw_k, k_gain), raw_k)
        query = jnp.where(lane >= HEAD_DIM, head_norm(raw_q, q_gain), 0.0).astype(BF)
        keyval = jnp.concatenate([raw[:, 0:128], key], axis=1).astype(BF)
        for p in range(2):
            for rb in range(4):
                at = unit(p, ra, rb)
                part = (p * 4 + rb) * HALF
                query_ref[pl.ds(pl.multiple_of(at * 16, 16), HALF), :] = query[part : part + HALF]
                kv[pl.ds(96 + at, 3)] = keyval[part : part + HALF].reshape(3, 16, 384)
                for way in range(2):
                    ship(kv.at[pl.ds(96 + at, 3)], kv.at[pl.ds(192 * way + at, 3)],
                         hsend.at[p, ra, rb, way], hrecv.at[p, ra, rb, way], at_z(1 - 2 * way))

    def halo(ra):
        for p in range(2):
            for rb in range(4):
                at = unit(p, ra, rb)
                for way in range(2):
                    wait_recv(kv.at[pl.ds(192 * way + at, 3)], hsend.at[0, 0, 0, 0], hrecv.at[p, ra, rb, way])

    def wout(ra, c, half):
        return wos.at[ra, pl.ds(c * 8, 8), pl.ds(pl.multiple_of(64 + half * 96, 32), 96), :]

    def wout_start():
        wos[0, :, 64:256, 128:256] = woq[:, :, 0:128]
        for c in range(2):
            for step, ra in ((1, 3), (-1, 1)):
                ship(wout(0, c, g), wout(ra, c, g), wsend.at[ra, c], wrecv.at[ra, c], at_xy(step, 0))

    def wout_got(ra, c):
        wait_recv(wout(ra, c, g), wsend.at[0, 0], wrecv.at[ra, c])
        if ra == 3 and c == 0:
            ship(wout(3, 0, g), wout(2, 0, g), wsend.at[2, 0], wrecv.at[2, 0], at_xy(1, 0))
        if ra == 1 and c == 1:
            ship(wout(1, 1, g), wout(2, 1, g), wsend.at[2, 1], wrecv.at[2, 1], at_xy(-1, 0))
        ship(wout(ra, c, g), wout(ra, c, g), vsend.at[ra, c], vrecv.at[ra, c], sibling())

    early, late = (0, 1, 2), (3,)
    weight_round(1, early)
    relay(4)
    start(0, 1)
    weight_round(2, early)
    near_rest(4)
    start(3, 0)
    weight_round(3, early)
    weight_round(4, early)
    relay(0)
    start(3, 1)
    weight_round(5, early)
    start(1, 0)
    weight_round(6, early)
    near_rest(0)
    relay(3)
    start(1, 1)
    weight_round(7, early)
    weight_round(8, early)
    far(4)
    far(0)
    weights_shared(early)
    group(0)
    start(2, 0)
    weight_round(1, late)
    weight_round(2, late)
    relay(1)
    start(2, 1)
    weight_round(3, late)
    weight_round(4, late)
    near_rest(3)
    far(3)
    group(3)
    weight_round(5, late)
    weight_round(6, late)
    relay(2)
    weight_round(7, late)
    near_rest(1)
    far(1)
    group(1)
    weight_round(8, late)
    weights_shared(late)
    near_rest(2)
    wout_start()
    far(2)
    group(2)
    halo(0)
    halo(3)
    lists.wait()
    counts.wait()

    key_lane = lax.broadcasted_iota(jnp.int32, (1, KT * 64), 1)
    slot = lax.rem(key_lane, 64)
    rank = lax.div(key_lane, 64)
    low_row = lax.div(slot, 8) < FRAME_H - 24
    low_col = lax.rem(slot, 8) < FRAME_W - 40
    row_slot = lax.broadcasted_iota(jnp.int32, (64, 1), 0)

    def attend_tile(tile):
        queries = query_ref[pl.ds(pl.multiple_of(tile * 64, 64), 64), :]
        stacked = jnp.concatenate(
            [jnp.where(lax.div(lane, 64) == h + 1, queries, jnp.zeros_like(queries)) for h in range(3)], axis=0
        )
        count = count_ref[tile]
        near = []
        row_last = jnp.zeros_like(key_lane)
        col_last = jnp.zeros_like(key_lane)
        for j in range(KT):
            index = jnp.clip(tiles_ref[tile, j] - (z - 1) * TILES, 0, 3 * TILES - 1)
            near += [kv[4 * index + i] for i in range(4)]
            within = lax.rem(index, TILES)
            here = rank == j
            row_last = jnp.where(here, (within >= 18).astype(jnp.int32), row_last)
            col_last = jnp.where(here, (lax.rem(within, TILES_W) == TILES_W - 1).astype(jnp.int32), col_last)
        near = jnp.concatenate(near, axis=0)
        keep = (rank < count) & ((row_last == 0) | low_row) & ((col_last == 0) | low_col)
        scores = lax.dot_general(
            stacked, near[:, 128:384], (((1,), (1,)), ((), ())), preferred_element_type=F32
        )
        scores = jnp.where(keep, scores, -1e30)
        top = jnp.max(scores, axis=-1, keepdims=True)
        weights = jnp.exp(scores - top).astype(BF)
        values = jnp.where(lane >= 192, jnp.ones((), BF), near[:, 0:256])
        mixed = jnp.dot(weights, values, preferred_element_type=F32)
        mixed = mixed / mixed[:, 192:193]
        result = jnp.where(
            lane < 64, mixed[0:64], jnp.where(lane < 128, mixed[64:128], mixed[128:192])
        )
        row, col = lax.div(tile, TILES_W), lax.rem(tile, TILES_W)
        alive = (row * 8 + lax.div(row_slot, 8) < FRAME_H) & (col * 8 + lax.rem(row_slot, 8) < FRAME_W)
        return jnp.where(alive, result, 0.0)

    def pack(left, right):
        right = pltpu.roll(right, 64, 1)
        middle = jnp.where(lane[:, 0:128] < 64, left[:, 128:256], right[:, 0:128])
        return jnp.concatenate([left[:, 0:128], middle, right[:, 128:256]], axis=1).astype(BF)

    def attend_row(k):
        row = lax.rem(x + k, SIDE)

        def one(i, carry):
            at = row * TILES_W + i
            att[k, pl.ds(pl.multiple_of(i * 64, 64), 64), :] = pack(attend_tile(at), attend_tile(at + 3))
            return carry

        lax.fori_loop(0, 3, one, 0)

    def mixed_piece(ra, rb, d):
        return gat.at[ra, rb, pl.ds(d * 96, 96), :]

    def start_y(ra):
        for k in range(2):
            for i, (d, step) in enumerate(WAYS):
                d = d ^ k
                src = att.at[0, pl.ds(d * 96, 96), :] if ra == 0 else mixed_piece(ra, 0, d)
                rb = 3 if step == 1 else 1
                ship(src, mixed_piece(ra, rb, d), ysend.at[ra, 2 * k + i], yrecv.at[ra, rb, d], at_xy(0, step))

    def got_y(ra, rb, d):
        wait_recv(mixed_piece(ra, rb, d), ysend.at[0, 0], yrecv.at[ra, rb, d])

    def relay_y(ra):
        for i, (d, step) in enumerate(WAYS):
            rb = 3 if step == 1 else 1
            got_y(ra, rb, d)
            ship(mixed_piece(ra, rb, d), mixed_piece(ra, 2, d), ysend.at[ra, 4 + i], yrecv.at[ra, 2, d],
                 at_xy(0, step))

    def rest_y(ra):
        got_y(ra, 3, 1)
        got_y(ra, 1, 0)
        got_y(ra, 2, 0)
        got_y(ra, 2, 1)

    def add_source(ra, rb, rows):
        h = lax.rem(x + ra, SIDE) * SIDE + lax.rem(y + rb, SIDE)
        for xi in range(4):
            acc[xi, 0:192, :] += jnp.dot(rows[:, 0:192], wos[xi, h, 64:256, :], preferred_element_type=F32)
            acc[xi, 192:384, :] += jnp.dot(rows[:, 128:384], wos[xi, h, :, :], preferred_element_type=F32)

    def add_row(ra, first):
        def one(rb, carry):
            add_source(ra, rb, gat[ra, rb])
            return carry

        lax.fori_loop(first, 4, one, 0)

    def start_x(k):
        ship(att.at[k], gat.at[4 - k, 0], asend.at[k], arecv.at[4 - k], at_xy(k, 0))

    def got_x(ra):
        wait_recv(gat.at[ra, 0], asend.at[0], arecv.at[ra])

    halo(1)
    halo(2)
    attend_row(0)
    start_y(0)
    attend_row(1)
    start_x(1)
    wout_got(3, 0)
    wout_got(1, 1)
    attend_row(3)
    start_x(3)
    wout_got(3, 1)
    wout_got(1, 0)
    relay_y(0)
    attend_row(2)
    start_x(2)
    drain()
    got_x(3)
    start_y(3)
    got_x(1)
    start_y(1)
    rest_y(0)
    relay_y(3)
    got_x(2)
    start_y(2)
    wout_got(2, 0)
    wout_got(2, 1)
    relay_y(1)
    for ra in range(1, 4):
        for c in range(2):
            wait_recv(wout(ra, c, 1 - g), vsend.at[0, 0], vrecv.at[ra, c])
    add_source(0, 0, att[0])
    add_row(0, 1)
    rest_y(3)
    relay_y(2)
    add_row(3, 0)
    rest_y(1)
    add_row(1, 0)
    drain()
    rest_y(2)
    add_row(2, 0)
    for xi in (2, 1, 3):
        outs[xi] = pack(acc[xi, 0:192, :], acc[xi, 192:384, :])
        ship(outs.at[xi], outs.at[8 - xi], osend.at[xi], orecv.at[4 - xi], at_xy(xi, 0))
    here = pl.multiple_of(x * 384, 384)
    out_ref[pl.ds(here, 384), :] = acc[0, :, 0:192].astype(BF)
    for ra in (3, 1, 2):
        wait_recv(outs.at[4 + ra], osend.at[0], orecv.at[ra])
        at = pl.multiple_of(lax.rem(x + ra, SIDE) * 384, 384)
        packed = outs[4 + ra]
        out_ref[pl.ds(at, 192), :] = packed[:, 0:192]
        right = pltpu.roll(packed[:, 128:384].astype(F32), 192, 1)
        out_ref[pl.ds(at + 192, 192), :] = right[:, 0:192].astype(BF)
    drain()


def on_device(tokens, w_query, w_key, w_value, w_out, q_gain, k_gain, key_tiles, key_count):
    vmem = pl.BlockSpec(memory_space=pltpu.VMEM)
    anywhere = pl.BlockSpec(memory_space=pl.ANY)
    sems = pltpu.SemaphoreType.DMA
    return pl.pallas_call(
        block_kernel,
        out_shape=jax.ShapeDtypeStruct((SLOTS, 192), BF),
        in_specs=[anywhere] * 2 + [vmem] * 7,
        out_specs=vmem,
        scratch_shapes=[
            pltpu.SMEM((TILES, KT), jnp.int32),
            pltpu.SMEM((TILES,), jnp.int32),
            pltpu.VMEM((4, 2, 4, HALF, D), BF),
            pltpu.VMEM((DEPTH, 192, 384), BF),
            pltpu.VMEM((DEPTH, 192, 256), BF),
            pltpu.VMEM((SLOTS, 256), BF),
            pltpu.VMEM((288, 16, 384), BF),
            pltpu.VMEM((4, DEPTH, 256, 256), BF),
            pltpu.VMEM((4, 192, 384), BF),
            pltpu.VMEM((4, 4, 192, 384), BF),
            pltpu.VMEM((4, 384, 256), F32),
            pltpu.VMEM((8, 192, 384), BF),
            sems((2,)),
            sems((2, 5, 6)), sems((2, 4, 4, 2)),
            sems((4, 2, 8)), sems((4, 2, 8)),
            sems((4, 2, 8)), sems((4, 2, 8)),
            sems((2, 4, 4, 2)), sems((2, 4, 4, 2)),
            sems((4, 2)), sems((4, 2)),
            sems((4, 2)), sems((4, 2)),
            sems((4,)), sems((4,)),
            sems((4, 6)), sems((4, 4, 2)),
            sems((4,)), sems((4,)),
        ],
        compiler_params=pltpu.CompilerParams(
            collective_id=0, has_side_effects=True, vmem_limit_bytes=56 * 1024 * 1024
        ),
        name="block_attention",
    )(key_tiles, key_count, tokens, w_query, w_key, w_value, w_out, q_gain[None, :], k_gain[None, :])


def solution(mesh):
    in_specs = (
        P(("guidance", "context", "head"), None),
        P("context", "head"),
        P("context", "head"),
        P("context", "head"),
        P("context", "head"),
        P(),
        P(),
        P("context", None),
        P("context"),
    )
    out_specs = P(("guidance", "context"), "head")
    return jax.shard_map(
        on_device, mesh=mesh, in_specs=in_specs, out_specs=out_specs, check_vma=False
    )
```

```python
import jax
import jax.numpy as jnp
from jax import lax
from jax.experimental import pallas as pl
from jax.experimental.pallas import tpu as pltpu
from jax.sharding import PartitionSpec as P

HEAD_DIM = 64
FRAME_H = 30
FRAME_W = 45
TILES_W = 6
TILES = 24
SLOTS = 1536
KT = 8
SIDE = 4
DEPTH = 16
D = 3072
MESH = pl.DeviceIdType.MESH
BF = jnp.bfloat16
F32 = jnp.float32


def place():
    g = lax.axis_index("guidance")
    z = lax.axis_index("context")
    h = lax.axis_index("head")
    return g, z, lax.div(h, SIDE), lax.rem(h, SIDE)


def at_xy(dx, dy):
    g, z, x, y = place()
    return (g, z, lax.rem(x + dx + SIDE, SIDE) * SIDE + lax.rem(y + dy + SIDE, SIDE))


def at_z(dz):
    g, z, x, y = place()
    return (g, lax.rem(z + dz + DEPTH, DEPTH), x * SIDE + y)


def sibling():
    g, z, x, y = place()
    return (1 - g, z, x * SIDE + y)


def send(src, dst, ssem, rsem, device):
    pltpu.make_async_remote_copy(
        src_ref=src, dst_ref=dst, send_sem=ssem, recv_sem=rsem, device_id=device, device_id_type=MESH
    ).start()


def wait_recv(dst, ssem, rsem):
    pltpu.make_async_remote_copy(
        src_ref=dst, dst_ref=dst, send_sem=ssem, recv_sem=rsem, device_id=sibling(), device_id_type=MESH
    ).wait_recv()


def wait_send(src, ssem, rsem):
    pltpu.make_async_remote_copy(
        src_ref=src, dst_ref=src, send_sem=ssem, recv_sem=rsem, device_id=sibling(), device_id_type=MESH
    ).wait_send()


def greet(partners):
    barrier = pltpu.get_barrier_semaphore()
    for partner in partners:
        pl.semaphore_signal(barrier, inc=1, device_id=partner, device_id_type=MESH)
    pl.semaphore_wait(barrier, len(partners))


def head_norm(raw, gain):
    lane_a = lax.broadcasted_iota(jnp.int32, (256, 256), 0) // HEAD_DIM
    lane_b = lax.broadcasted_iota(jnp.int32, (256, 256), 1) // HEAD_DIM
    pick = jnp.where(lane_a == lane_b, 1.0 / HEAD_DIM, 0.0).astype(BF)

    def mean(values):
        high = values.astype(BF)
        low = (values - high.astype(F32)).astype(BF)
        return jnp.dot(high, pick, preferred_element_type=F32) + jnp.dot(
            low, pick, preferred_element_type=F32
        )

    centred = raw - mean(raw)
    spread = mean(centred * centred)
    return centred * lax.rsqrt(spread + 1e-06) * gain


HALF = 48
COLS = D // 2
WAYS = ((0, 1), (1, -1))
STREAMS = 3
ORDER = (0, 3, 1, 2)
SLOT = {0: 0, 3: 1, 1: 2}


def block_kernel(
    tiles_hbm, count_hbm, tok_ref, wq_ref, wk_ref, wv_ref, wo_ref, qg_ref, kg_ref,
    out_ref,
    tiles_ref, count_ref, close, distant, wall, query_ref, kv, wos, att, gat, acc, outs,
    csem, tsend, trecv, zsend, zrecv, ssend, srecv, hsend, hrecv,
    wsend, wrecv, vsend, vrecv, asend, arecv, ysend, yrecv, osend, orecv,
):
    g, z, x, y = place()
    lists = pltpu.make_async_copy(tiles_hbm, tiles_ref, csem.at[0])
    counts = pltpu.make_async_copy(count_hbm, count_ref, csem.at[1])
    lists.start()
    counts.start()
    greet([
        at_xy(1, 0), at_xy(-1, 0), at_xy(2, 0), at_xy(0, 1), at_xy(0, -1), at_z(1), at_z(-1), sibling()
    ])
    sent = []

    def ship(src, dst, ssem, rsem, device):
        send(src, dst, ssem, rsem, device)
        sent.append((src, ssem, rsem))

    def drain():
        for src, ssem, rsem in sent:
            wait_send(src, ssem, rsem)
        sent.clear()

    def axis_dev(p, second, step):
        along_x = (p == 0) != second
        return at_xy(step, 0) if along_x else at_xy(0, step)

    def piece(p, ra, rb, d):
        at = ORDER.index(ra)
        here = distant.at[at, p] if rb == 2 else close.at[at, p, SLOT[rb]]
        return here.at[:, pl.ds(d * COLS, COLS)]

    def landing(p, rnd, rel, d):
        return piece(p, rel, 0, d) if rnd == 4 else piece(p, rnd, rel, d)

    def own(p, d):
        return tok_ref.at[pl.ds(p * HALF, HALF), pl.ds(d * COLS, COLS)]

    def arrival(p, rnd, rel, d):
        return trecv.at[p, rel, 0, d] if rnd == 4 else trecv.at[p, rnd, rel, d]

    def start(rnd, k):
        for p in range(2):
            for i, (d, step) in enumerate(WAYS):
                d = d ^ k
                src = own(p, d) if rnd in (0, 4) else piece(p, rnd, 0, d)
                rel = 3 if step == 1 else 1
                ship(src, landing(p, rnd, rel, d), tsend.at[p, rnd, 2 * k + i], arrival(p, rnd, rel, d),
                     axis_dev(p, rnd != 4, step))

    def got(p, rnd, rel, d):
        wait_recv(landing(p, rnd, rel, d), tsend.at[p, 0, 0], arrival(p, rnd, rel, d))

    def relay(rnd):
        for p in range(2):
            for i, (d, step) in enumerate(WAYS):
                rel = 3 if step == 1 else 1
                got(p, rnd, rel, d)
                ship(landing(p, rnd, rel, d), landing(p, rnd, 2, d), tsend.at[p, rnd, 4 + i],
                     arrival(p, rnd, 2, d), axis_dev(p, rnd != 4, step))

    def near_rest(rnd):
        for p in range(2):
            got(p, rnd, 3, 1)
            got(p, rnd, 1, 0)

    def far(rnd):
        for p in range(2):
            got(p, rnd, 2, 0)
            got(p, rnd, 2, 1)

    def block(stream, dz, half):
        at = lax.rem(z + dz + DEPTH, DEPTH)
        return wall.at[at, pl.ds(pl.multiple_of(half * 96, 96), 96), pl.ds(stream * 256, 256)]

    def steps(stream, way):
        return 8 if (stream + way) % 2 == 0 else 7

    def ship_weights(stream, way, s):
        dz = -s if way == 0 else s
        ship(block(stream, dz, g), block(stream, dz, g), zsend.at[stream, way, s], zrecv.at[stream, way, s],
             at_z(1 if way == 0 else -1))

    def ship_stream(stream):
        for way in range(2):
            ship_weights(stream, way, 0)

    def weight_round(s):
        for stream in range(STREAMS):
            for way in range(2):
                if s > steps(stream, way):
                    continue
                dz = -s if way == 0 else s
                here = block(stream, dz, g)
                wait_recv(here, zsend.at[stream, way, 0], zrecv.at[stream, way, s - 1])
                if s < steps(stream, way):
                    ship_weights(stream, way, s)
                ship(here, here, ssend.at[stream, way, s - 1], srecv.at[stream, way, s - 1], sibling())

    def weights_shared():
        for stream in range(STREAMS):
            for way in range(2):
                for s in range(1, steps(stream, way) + 1):
                    dz = -s if way == 0 else s
                    wait_recv(block(stream, dz, 1 - g), ssend.at[stream, way, 0], srecv.at[stream, way, s - 1])

    start(4, 0)
    wall[z, :, 0:384] = jnp.concatenate([wv_ref[...], wk_ref[...]], axis=1)
    ship_stream(0)
    start(4, 1)
    wall[z, :, 384:768] = jnp.concatenate([wo_ref[...], wq_ref[...]], axis=1)
    ship_stream(1)
    for p in range(2):
        close[0, p, 0] = tok_ref[pl.ds(p * HALF, HALF), :]
    wos[:, :, 0:64, :] = jnp.zeros((4, DEPTH, 64, 256), BF)
    ship_stream(2)
    start(0, 0)

    lane = lax.broadcasted_iota(jnp.int32, (1, 256), 1)
    q_gain = jnp.concatenate([qg_ref[...]] * 4, axis=1) * 0.125
    k_gain = jnp.concatenate([kg_ref[...]] * 4, axis=1)

    def unit(p, ra, rb):
        a_x, a_y = (ra, rb) if p == 0 else (rb, ra)
        return lax.rem(x + a_x, SIDE) * 24 + lax.rem(y + a_y, SIDE) * 6 + p * 3

    def group(rows, pieces):
        raw = jnp.dot(rows, wall[:, :, 0:384].reshape(D, 384), preferred_element_type=F32)
        raw_q = jnp.dot(rows, wall[:, :, 512:768].reshape(D, 256), preferred_element_type=F32)
        raw_k = raw[:, 128:384]
        key = jnp.where(lane >= HEAD_DIM, head_norm(raw_k, k_gain), raw_k)
        query = jnp.where(lane >= HEAD_DIM, head_norm(raw_q, q_gain), 0.0).astype(BF)
        keyval = jnp.concatenate([raw[:, 0:128], key], axis=1).astype(BF)
        for i, (p, ra, rb) in enumerate(pieces):
            at = unit(p, ra, rb)
            part = slice(i * HALF, (i + 1) * HALF)
            query_ref[pl.ds(pl.multiple_of(at * 16, 16), HALF), :] = query[part]
            kv[pl.ds(96 + at, 3)] = keyval[part].reshape(3, 16, 384)
            for way in range(2):
                ship(kv.at[pl.ds(96 + at, 3)], kv.at[pl.ds(192 * way + at, 3)],
                     hsend.at[p, ra, rb, way], hrecv.at[p, ra, rb, way], at_z(1 - 2 * way))

    def near_group(ra):
        group(close[ORDER.index(ra)].reshape(6 * HALF, D), [(p, ra, rb) for p in range(2) for rb in SLOT])

    def far_group(first, last):
        group(distant[first:last].reshape((last - first) * 2 * HALF, D),
              [(p, ORDER[at], 2) for at in range(first, last) for p in range(2)])

    def halo(ra):
        for p in range(2):
            for rb in range(4):
                at = unit(p, ra, rb)
                for way in range(2):
                    wait_recv(kv.at[pl.ds(192 * way + at, 3)], hsend.at[0, 0, 0, 0], hrecv.at[p, ra, rb, way])

    def wout(ra, c, half):
        return wos.at[ra, pl.ds(c * 8, 8), pl.ds(pl.multiple_of(64 + half * 96, 32), 96), :]

    def wout_start():
        wos[0, :, 64:256, :] = wall[:, :, 384:640]
        for c in range(2):
            for step, ra in ((1, 3), (-1, 1)):
                ship(wout(0, c, g), wout(ra, c, g), wsend.at[ra, c], wrecv.at[ra, c], at_xy(step, 0))

    def wout_got(ra, c):
        wait_recv(wout(ra, c, g), wsend.at[0, 0], wrecv.at[ra, c])
        if ra == 3 and c == 0:
            ship(wout(3, 0, g), wout(2, 0, g), wsend.at[2, 0], wrecv.at[2, 0], at_xy(1, 0))
        if ra == 1 and c == 1:
            ship(wout(1, 1, g), wout(2, 1, g), wsend.at[2, 1], wrecv.at[2, 1], at_xy(-1, 0))
        ship(wout(ra, c, g), wout(ra, c, g), vsend.at[ra, c], vrecv.at[ra, c], sibling())

    weight_round(1)
    relay(4)
    start(0, 1)
    weight_round(2)
    near_rest(4)
    start(3, 0)
    weight_round(3)
    relay(0)
    start(3, 1)
    start(1, 0)
    weight_round(4)
    weight_round(5)
    weight_round(6)
    relay(3)
    start(1, 1)
    far(4)
    start(2, 0)
    weight_round(7)
    weight_round(8)
    weights_shared()
    near_rest(0)
    near_group(0)
    relay(1)
    start(2, 1)
    near_rest(3)
    near_group(3)
    near_rest(1)
    near_group(1)
    relay(2)
    far(0)
    far(3)
    far(1)
    far_group(0, 3)
    near_rest(2)
    wout_start()
    near_group(2)
    far(2)
    far_group(3, 4)
    lists.wait()
    counts.wait()

    key_lane = lax.broadcasted_iota(jnp.int32, (1, KT * 64), 1)
    slot = lax.rem(key_lane, 64)
    rank = lax.div(key_lane, 64)
    low_row = lax.div(slot, 8) < FRAME_H - 24
    low_col = lax.rem(slot, 8) < FRAME_W - 40
    row_slot = lax.broadcasted_iota(jnp.int32, (64, 1), 0)

    def attend_tile(tile):
        queries = query_ref[pl.ds(pl.multiple_of(tile * 64, 64), 64), :]
        stacked = jnp.concatenate(
            [jnp.where(lax.div(lane, 64) == h + 1, queries, jnp.zeros_like(queries)) for h in range(3)], axis=0
        )
        count = count_ref[tile]
        near = []
        row_last = jnp.zeros_like(key_lane)
        col_last = jnp.zeros_like(key_lane)
        for j in range(KT):
            index = jnp.clip(tiles_ref[j, tile] - (z - 1) * TILES, 0, 3 * TILES - 1)
            near += [kv[4 * index + i] for i in range(4)]
            within = lax.rem(index, TILES)
            here = rank == j
            row_last = jnp.where(here, (within >= 18).astype(jnp.int32), row_last)
            col_last = jnp.where(here, (lax.rem(within, TILES_W) == TILES_W - 1).astype(jnp.int32), col_last)
        near = jnp.concatenate(near, axis=0)
        keep = (rank < count) & ((row_last == 0) | low_row) & ((col_last == 0) | low_col)
        scores = lax.dot_general(
            stacked, near[:, 128:384], (((1,), (1,)), ((), ())), preferred_element_type=F32
        )
        scores = jnp.where(keep, scores, -1e30)
        top = jnp.max(scores, axis=-1, keepdims=True)
        weights = jnp.exp(scores - top).astype(BF)
        values = jnp.where(lane >= 192, jnp.ones((), BF), near[:, 0:256])
        mixed = jnp.dot(weights, values, preferred_element_type=F32)
        mixed = mixed / mixed[:, 192:193]
        result = jnp.where(
            lane < 64, mixed[0:64], jnp.where(lane < 128, mixed[64:128], mixed[128:192])
        )
        row, col = lax.div(tile, TILES_W), lax.rem(tile, TILES_W)
        alive = (row * 8 + lax.div(row_slot, 8) < FRAME_H) & (col * 8 + lax.rem(row_slot, 8) < FRAME_W)
        return jnp.where(alive, result, 0.0)

    def pack(left, right):
        right = pltpu.roll(right, 64, 1)
        middle = jnp.where(lane[:, 0:128] < 64, left[:, 128:256], right[:, 0:128])
        return jnp.concatenate([left[:, 0:128], middle, right[:, 128:256]], axis=1).astype(BF)

    def attend_row(k):
        row = lax.rem(x + k, SIDE)

        def one(i, carry):
            at = row * TILES_W + i
            att[k, pl.ds(pl.multiple_of(i * 64, 64), 64), :] = pack(attend_tile(at), attend_tile(at + 3))
            return carry

        lax.fori_loop(0, 3, one, 0)

    def mixed_piece(ra, rb, d):
        return gat.at[ra, rb, pl.ds(d * 96, 96), :]

    def start_y(ra):
        for k in range(2):
            for i, (d, step) in enumerate(WAYS):
                d = d ^ k
                src = att.at[0, pl.ds(d * 96, 96), :] if ra == 0 else mixed_piece(ra, 0, d)
                rb = 3 if step == 1 else 1
                ship(src, mixed_piece(ra, rb, d), ysend.at[ra, 2 * k + i], yrecv.at[ra, rb, d], at_xy(0, step))

    def got_y(ra, rb, d):
        wait_recv(mixed_piece(ra, rb, d), ysend.at[0, 0], yrecv.at[ra, rb, d])

    def relay_y(ra):
        for i, (d, step) in enumerate(WAYS):
            rb = 3 if step == 1 else 1
            got_y(ra, rb, d)
            ship(mixed_piece(ra, rb, d), mixed_piece(ra, 2, d), ysend.at[ra, 4 + i], yrecv.at[ra, 2, d],
                 at_xy(0, step))

    def rest_y(ra):
        got_y(ra, 3, 1)
        got_y(ra, 1, 0)
        got_y(ra, 2, 0)
        got_y(ra, 2, 1)

    def add_source(ra, rb, rows, first=False):
        h = lax.rem(x + ra, SIDE) * SIDE + lax.rem(y + rb, SIDE)
        for xi in range(4):
            top = jnp.dot(rows[:, 0:192], wos[xi, h, 64:256, :], preferred_element_type=F32)
            low = jnp.dot(rows[:, 128:384], wos[xi, h, :, :], preferred_element_type=F32)
            if first:
                acc[xi, 0:192, :] = top
                acc[xi, 192:384, :] = low
            else:
                acc[xi, 0:192, :] += top
                acc[xi, 192:384, :] += low

    def add_row(ra, first):
        def one(rb, carry):
            add_source(ra, rb, gat[ra, rb])
            return carry

        lax.fori_loop(first, 4, one, 0)

    def start_x(k):
        ship(att.at[k], gat.at[4 - k, 0], asend.at[k], arecv.at[4 - k], at_xy(k, 0))

    def got_x(ra):
        wait_recv(gat.at[ra, 0], asend.at[0], arecv.at[ra])

    for ra in ORDER:
        halo(ra)
    attend_row(0)
    start_y(0)
    attend_row(1)
    start_x(1)
    attend_row(3)
    start_x(3)
    relay_y(0)
    attend_row(2)
    start_x(2)
    wout_got(3, 0)
    wout_got(1, 1)
    got_x(3)
    start_y(3)
    got_x(1)
    start_y(1)
    drain()
    wout_got(3, 1)
    wout_got(1, 0)
    rest_y(0)
    relay_y(3)
    got_x(2)
    start_y(2)
    relay_y(1)
    wout_got(2, 0)
    wout_got(2, 1)
    for ra in range(1, 4):
        for c in range(2):
            wait_recv(wout(ra, c, 1 - g), vsend.at[0, 0], vrecv.at[ra, c])
    add_source(0, 0, att[0], True)
    add_row(0, 1)
    rest_y(3)
    relay_y(2)
    add_row(3, 0)
    rest_y(1)
    add_row(1, 0)
    drain()
    rest_y(2)
    add_row(2, 0)
    def result(xs):
        return out_ref.at[:, pl.ds(pl.multiple_of(xs * 384, 128), 384)]

    for xi in (2, 1, 3):
        outs[xi] = acc[xi].T[0:192].astype(BF)
        ship(outs.at[xi], result(x), osend.at[xi], orecv.at[4 - xi], at_xy(xi, 0))
    out_ref[:, pl.ds(pl.multiple_of(x * 384, 128), 384)] = acc[0].T[0:192].astype(BF)
    for ra in (3, 1, 2):
        wait_recv(result(lax.rem(x + ra, SIDE)), osend.at[0], orecv.at[ra])
    drain()


def on_device(tokens, w_query, w_key, w_value, w_out, q_gain, k_gain, key_tiles, key_count):
    vmem = pl.BlockSpec(memory_space=pltpu.VMEM)
    anywhere = pl.BlockSpec(memory_space=pl.ANY)
    sems = pltpu.SemaphoreType.DMA
    return pl.pallas_call(
        block_kernel,
        out_shape=jax.ShapeDtypeStruct((192, SLOTS), BF),
        in_specs=[anywhere] * 2 + [vmem] * 7,
        out_specs=vmem,
        scratch_shapes=[
            pltpu.SMEM((KT, TILES), jnp.int32),
            pltpu.SMEM((TILES,), jnp.int32),
            pltpu.VMEM((4, 2, 3, HALF, D), BF),
            pltpu.VMEM((4, 2, HALF, D), BF),
            pltpu.VMEM((DEPTH, 192, 768), BF),
            pltpu.VMEM((SLOTS, 256), BF),
            pltpu.VMEM((288, 16, 384), BF),
            pltpu.VMEM((4, DEPTH, 256, 256), BF),
            pltpu.VMEM((4, 192, 384), BF),
            pltpu.VMEM((4, 4, 192, 384), BF),
            pltpu.VMEM((4, 384, 256), F32),
            pltpu.VMEM((4, 192, 384), BF),
            sems((2,)),
            sems((2, 5, 6)), sems((2, 4, 4, 2)),
            sems((STREAMS, 2, 8)), sems((STREAMS, 2, 8)),
            sems((STREAMS, 2, 8)), sems((STREAMS, 2, 8)),
            sems((2, 4, 4, 2)), sems((2, 4, 4, 2)),
            sems((4, 2)), sems((4, 2)),
            sems((4, 2)), sems((4, 2)),
            sems((4,)), sems((4,)),
            sems((4, 6)), sems((4, 4, 2)),
            sems((4,)), sems((4,)),
        ],
        compiler_params=pltpu.CompilerParams(
            collective_id=0, has_side_effects=True, vmem_limit_bytes=56 * 1024 * 1024
        ),
        name="block_attention",
    )(key_tiles.T, key_count, tokens, w_query, w_key, w_value, w_out, q_gain[None, :], k_gain[None, :]).T


def solution(mesh):
    in_specs = (
        P(("guidance", "context", "head"), None),
        P("context", "head"),
        P("context", "head"),
        P("context", "head"),
        P("context", "head"),
        P(),
        P(),
        P("context", None),
        P("context"),
    )
    out_specs = P(("guidance", "context"), "head")
    return jax.shard_map(
        on_device, mesh=mesh, in_specs=in_specs, out_specs=out_specs, check_vma=False
    )
```

```python
import jax
import jax.numpy as jnp
from jax import lax
from jax.experimental import pallas as pl
from jax.experimental.pallas import tpu as pltpu
from jax.sharding import PartitionSpec as P

HEAD_DIM = 64
FRAME_H = 30
FRAME_W = 45
TILES_W = 6
TILES = 24
SLOTS = 1536
KT = 8
SIDE = 4
DEPTH = 16
D = 3072
MESH = pl.DeviceIdType.MESH
BF = jnp.bfloat16
F32 = jnp.float32


def place():
    g = lax.axis_index("guidance")
    z = lax.axis_index("context")
    h = lax.axis_index("head")
    return g, z, lax.div(h, SIDE), lax.rem(h, SIDE)


def at_xy(dx, dy):
    g, z, x, y = place()
    return (g, z, lax.rem(x + dx + SIDE, SIDE) * SIDE + lax.rem(y + dy + SIDE, SIDE))


def at_z(dz):
    g, z, x, y = place()
    return (g, lax.rem(z + dz + DEPTH, DEPTH), x * SIDE + y)


def sibling():
    g, z, x, y = place()
    return (1 - g, z, x * SIDE + y)


def send(src, dst, ssem, rsem, device):
    pltpu.make_async_remote_copy(
        src_ref=src, dst_ref=dst, send_sem=ssem, recv_sem=rsem, device_id=device, device_id_type=MESH
    ).start()


def wait_recv(dst, ssem, rsem):
    pltpu.make_async_remote_copy(
        src_ref=dst, dst_ref=dst, send_sem=ssem, recv_sem=rsem, device_id=sibling(), device_id_type=MESH
    ).wait_recv()


def wait_send(src, ssem, rsem):
    pltpu.make_async_remote_copy(
        src_ref=src, dst_ref=src, send_sem=ssem, recv_sem=rsem, device_id=sibling(), device_id_type=MESH
    ).wait_send()


def greet(partners):
    barrier = pltpu.get_barrier_semaphore()
    for partner in partners:
        pl.semaphore_signal(barrier, inc=1, device_id=partner, device_id_type=MESH)
    pl.semaphore_wait(barrier, len(partners))


def head_norm(raw, gain):
    lane_a = lax.broadcasted_iota(jnp.int32, (256, 256), 0) // HEAD_DIM
    lane_b = lax.broadcasted_iota(jnp.int32, (256, 256), 1) // HEAD_DIM
    pick = jnp.where(lane_a == lane_b, 1.0 / HEAD_DIM, 0.0).astype(BF)

    def mean(values):
        high = values.astype(BF)
        low = (values - high.astype(F32)).astype(BF)
        return jnp.dot(high, pick, preferred_element_type=F32) + jnp.dot(
            low, pick, preferred_element_type=F32
        )

    centred = raw - mean(raw)
    spread = mean(centred * centred)
    return centred * lax.rsqrt(spread + 1e-06) * gain


HALF = 48
COLS = D // 2
WAYS = ((0, 1), (1, -1))
STREAMS = 6
ORDER = (0, 3, 1, 2)
SLOT = {0: 0, 3: 1, 1: 2}


def block_kernel(
    tiles_hbm, count_hbm, tok_ref, wq_ref, wk_ref, wv_ref, wo_ref, qg_ref, kg_ref,
    out_ref,
    tiles_ref, count_ref, close, distant, wall, query_ref, kv, wos, pairs, att, gat, acc, outs,
    csem, tsend, trecv, zsend, zrecv, ssend, srecv, hsend, hrecv,
    wsend, wrecv, vsend, vrecv, asend, arecv, ysend, yrecv, osend, orecv,
):
    g, z, x, y = place()
    lists = pltpu.make_async_copy(tiles_hbm, tiles_ref, csem.at[0])
    counts = pltpu.make_async_copy(count_hbm, count_ref, csem.at[1])
    lists.start()
    counts.start()
    greet([
        at_xy(1, 0), at_xy(-1, 0), at_xy(2, 0), at_xy(0, 1), at_xy(0, -1), at_z(1), at_z(-1), sibling()
    ])
    sent = []

    def ship(src, dst, ssem, rsem, device):
        send(src, dst, ssem, rsem, device)
        sent.append((src, ssem, rsem))

    def drain():
        for src, ssem, rsem in sent:
            wait_send(src, ssem, rsem)
        sent.clear()

    def axis_dev(p, second, step):
        along_x = (p == 0) != second
        return at_xy(step, 0) if along_x else at_xy(0, step)

    def piece(p, ra, rb, d):
        at = ORDER.index(ra)
        here = distant.at[at, p] if rb == 2 else close.at[at, p, SLOT[rb]]
        return here.at[:, pl.ds(d * COLS, COLS)]

    def landing(p, rnd, rel, d):
        return piece(p, rel, 0, d) if rnd == 4 else piece(p, rnd, rel, d)

    def own(p, d):
        return tok_ref.at[pl.ds(p * HALF, HALF), pl.ds(d * COLS, COLS)]

    def arrival(p, rnd, rel, d):
        return trecv.at[p, rel, 0, d] if rnd == 4 else trecv.at[p, rnd, rel, d]

    def start(rnd, k):
        for p in range(2):
            for i, (d, step) in enumerate(WAYS):
                d = d ^ k
                src = own(p, d) if rnd in (0, 4) else piece(p, rnd, 0, d)
                rel = 3 if step == 1 else 1
                ship(src, landing(p, rnd, rel, d), tsend.at[p, rnd, 2 * k + i], arrival(p, rnd, rel, d),
                     axis_dev(p, rnd != 4, step))

    def got(p, rnd, rel, d):
        wait_recv(landing(p, rnd, rel, d), tsend.at[p, 0, 0], arrival(p, rnd, rel, d))

    def relay(rnd):
        for p in range(2):
            for i, (d, step) in enumerate(WAYS):
                rel = 3 if step == 1 else 1
                got(p, rnd, rel, d)
                ship(landing(p, rnd, rel, d), landing(p, rnd, 2, d), tsend.at[p, rnd, 4 + i],
                     arrival(p, rnd, 2, d), axis_dev(p, rnd != 4, step))

    def near_rest(rnd):
        for p in range(2):
            got(p, rnd, 3, 1)
            got(p, rnd, 1, 0)

    def far(rnd):
        for p in range(2):
            got(p, rnd, 2, 0)
            got(p, rnd, 2, 1)

    def block(stream, dz, half):
        at = lax.rem(z + dz + DEPTH, DEPTH)
        rows = pl.ds(pl.multiple_of(half * 96 + stream % 2 * 48, 16), 48)
        return wall.at[at, rows, pl.ds(stream // 2 * 256, 256)]

    def steps(stream, way):
        return 8 if (stream + way) % 2 == 0 else 7

    def ship_weights(stream, way, s):
        dz = -s if way == 0 else s
        ship(block(stream, dz, g), block(stream, dz, g), zsend.at[stream, way, s], zrecv.at[stream, way, s],
             at_z(1 if way == 0 else -1))

    def ship_stream(stream):
        for way in range(2):
            ship_weights(stream, way, 0)

    def weight_round(s):
        for stream in range(STREAMS):
            for way in range(2):
                if s > steps(stream, way):
                    continue
                dz = -s if way == 0 else s
                here = block(stream, dz, g)
                wait_recv(here, zsend.at[stream, way, 0], zrecv.at[stream, way, s - 1])
                if s < steps(stream, way):
                    ship_weights(stream, way, s)
                ship(here, here, ssend.at[stream, way, s - 1], srecv.at[stream, way, s - 1], sibling())

    def weights_shared():
        for stream in range(STREAMS):
            for way in range(2):
                for s in range(1, steps(stream, way) + 1):
                    dz = -s if way == 0 else s
                    wait_recv(block(stream, dz, 1 - g), ssend.at[stream, way, 0], srecv.at[stream, way, s - 1])

    start(4, 0)
    wall[z, :, 0:384] = jnp.concatenate([wv_ref[...], wk_ref[...]], axis=1)
    ship_stream(0)
    ship_stream(1)
    start(4, 1)
    wall[z, :, 384:768] = jnp.concatenate([wo_ref[...], wq_ref[...]], axis=1)
    ship_stream(2)
    ship_stream(3)
    for p in range(2):
        close[0, p, 0] = tok_ref[pl.ds(p * HALF, HALF), :]
    wos[:, :, 0:64, :] = jnp.zeros((4, DEPTH, 64, 256), BF)
    ship_stream(4)
    ship_stream(5)

    lane = lax.broadcasted_iota(jnp.int32, (1, 256), 1)
    q_gain = jnp.concatenate([qg_ref[...]] * 4, axis=1) * 0.125
    k_gain = jnp.concatenate([kg_ref[...]] * 4, axis=1)

    def unit(p, ra, rb):
        a_x, a_y = (ra, rb) if p == 0 else (rb, ra)
        return lax.rem(x + a_x, SIDE) * 24 + lax.rem(y + a_y, SIDE) * 6 + p * 3

    def group(rows, pieces):
        raw = jnp.dot(rows, wall[:, :, 0:384].reshape(D, 384), preferred_element_type=F32)
        raw_q = jnp.dot(rows, wall[:, :, 512:768].reshape(D, 256), preferred_element_type=F32)
        raw_k = raw[:, 128:384]
        key = jnp.where(lane >= HEAD_DIM, head_norm(raw_k, k_gain), raw_k)
        query = jnp.where(lane >= HEAD_DIM, head_norm(raw_q, q_gain), 0.0).astype(BF)
        keyval = jnp.concatenate([raw[:, 0:128], key], axis=1).astype(BF)
        for i, (p, ra, rb) in enumerate(pieces):
            at = unit(p, ra, rb)
            part = slice(i * HALF, (i + 1) * HALF)
            query_ref[pl.ds(pl.multiple_of(at * 16, 16), HALF), :] = query[part]
            kv[pl.ds(96 + at, 3)] = keyval[part].reshape(3, 16, 384)
            for way in range(2):
                ship(kv.at[pl.ds(96 + at, 3)], kv.at[pl.ds(192 * way + at, 3)],
                     hsend.at[p, ra, rb, way], hrecv.at[p, ra, rb, way], at_z(1 - 2 * way))

    def near_group(ra):
        group(close[ORDER.index(ra)].reshape(6 * HALF, D), [(p, ra, rb) for p in range(2) for rb in SLOT])

    def far_group(first, last):
        group(distant[first:last].reshape((last - first) * 2 * HALF, D),
              [(p, ORDER[at], 2) for at in range(first, last) for p in range(2)])

    def halo(ra):
        for p in range(2):
            for rb in range(4):
                at = unit(p, ra, rb)
                for way in range(2):
                    wait_recv(kv.at[pl.ds(192 * way + at, 3)], hsend.at[0, 0, 0, 0], hrecv.at[p, ra, rb, way])

    def wout(ra, c, half):
        if c < 4:
            rows = pl.ds(pl.multiple_of(64 + half * 96, 32), 96)
            return wos.at[ra, pl.ds(c * 4, 4), rows, pl.ds(0, 128)]
        return pairs.at[ra, pl.ds((c - 4) * 4, 4), pl.ds(pl.multiple_of(half * 96, 32), 96), :]

    def swap(block):
        return pltpu.roll(block.astype(F32).reshape(8 * 192, 128), 64, 1).reshape(8, 192, 128).astype(BF)

    def wout_own():
        wos[0, :, 64:256, :] = wall[:, :, 384:640]
        lower = lane[:, 0:128].reshape(1, 1, 128) < 64
        pairs[0] = jnp.where(lower, wall[0:8, :, 512:640], swap(wall[8:16, :, 512:640]))

    def wout_start(k):
        for c in range(6):
            step, ra = ((1, 3), (-1, 1))[(c in (2, 3, 5)) ^ k]
            ship(wout(0, c, g), wout(ra, c, g), wsend.at[ra, c], wrecv.at[ra, c], at_xy(step, 0))

    def wout_pass(ra, c):
        wait_recv(wout(ra, c, g), wsend.at[0, 0], wrecv.at[ra, c])
        ship(wout(ra, c, g), wout(ra, c, g), vsend.at[ra, c], vrecv.at[ra, c], sibling())

    def wout_relay():
        for c in range(6):
            step, ra = ((1, 3), (-1, 1))[c in (2, 3, 5)]
            wout_pass(ra, c)
            ship(wout(ra, c, g), wout(2, c, g), wsend.at[2, c], wrecv.at[2, c], at_xy(step, 0))

    def wout_rest():
        for c in range(6):
            wout_pass(1 if c in (0, 1, 4) else 3, c)
        for c in range(6):
            wout_pass(2, c)

    def wout_finish():
        for ra in range(1, 4):
            for c in range(6):
                wait_recv(wout(ra, c, 1 - g), vsend.at[0, 0], vrecv.at[ra, c])
            wos[ra, 0:8, 64:256, 128:256] = pairs[ra]
            wos[ra, 8:16, 64:256, 128:256] = swap(pairs[ra])

    weight_round(1)
    start(0, 0)
    relay(4)
    near_rest(4)
    start(0, 1)
    start(3, 0)
    weight_round(2)
    weight_round(3)
    relay(0)
    start(3, 1)
    start(1, 0)
    weight_round(4)
    weight_round(5)
    weight_round(6)
    far(4)
    relay(3)
    start(1, 1)
    start(2, 0)
    weight_round(7)
    weight_round(8)
    weights_shared()
    near_rest(0)
    near_group(0)
    relay(1)
    start(2, 1)
    near_rest(3)
    near_group(3)
    near_rest(1)
    near_group(1)
    relay(2)
    wout_own()
    wout_start(0)
    far(0)
    far(3)
    far(1)
    far_group(0, 3)
    near_rest(2)
    near_group(2)
    far(2)
    wout_relay()
    wout_start(1)
    far_group(3, 4)
    for ra in ORDER:
        halo(ra)
    lists.wait()
    counts.wait()

    key_lane = lax.broadcasted_iota(jnp.int32, (1, KT * 64), 1)
    slot = lax.rem(key_lane, 64)
    rank = lax.div(key_lane, 64)
    low_row = lax.div(slot, 8) < FRAME_H - 24
    low_col = lax.rem(slot, 8) < FRAME_W - 40
    row_slot = lax.broadcasted_iota(jnp.int32, (64, 1), 0)

    def attend_tile(tile):
        queries = query_ref[pl.ds(pl.multiple_of(tile * 64, 64), 64), :]
        stacked = jnp.concatenate(
            [jnp.where(lax.div(lane, 64) == h + 1, queries, jnp.zeros_like(queries)) for h in range(3)], axis=0
        )
        count = count_ref[tile]
        near = []
        row_last = jnp.zeros_like(key_lane)
        col_last = jnp.zeros_like(key_lane)
        for j in range(KT):
            index = jnp.clip(tiles_ref[j, tile] - (z - 1) * TILES, 0, 3 * TILES - 1)
            near += [kv[4 * index + i] for i in range(4)]
            within = lax.rem(index, TILES)
            here = rank == j
            row_last = jnp.where(here, (within >= 18).astype(jnp.int32), row_last)
            col_last = jnp.where(here, (lax.rem(within, TILES_W) == TILES_W - 1).astype(jnp.int32), col_last)
        near = jnp.concatenate(near, axis=0)
        keep = (rank < count) & ((row_last == 0) | low_row) & ((col_last == 0) | low_col)
        scores = lax.dot_general(
            stacked, near[:, 128:384], (((1,), (1,)), ((), ())), preferred_element_type=F32
        )
        scores = jnp.where(keep, scores, -1e30)
        top = jnp.max(scores, axis=-1, keepdims=True)
        weights = jnp.exp(scores - top).astype(BF)
        values = jnp.where(lane >= 192, jnp.ones((), BF), near[:, 0:256])
        mixed = jnp.dot(weights, values, preferred_element_type=F32)
        mixed = mixed / mixed[:, 192:193]
        result = jnp.where(
            lane < 64, mixed[0:64], jnp.where(lane < 128, mixed[64:128], mixed[128:192])
        )
        row, col = lax.div(tile, TILES_W), lax.rem(tile, TILES_W)
        alive = (row * 8 + lax.div(row_slot, 8) < FRAME_H) & (col * 8 + lax.rem(row_slot, 8) < FRAME_W)
        return jnp.where(alive, result, 0.0)

    def pack(left, right):
        right = pltpu.roll(right, 64, 1)
        middle = jnp.where(lane[:, 0:128] < 64, left[:, 128:256], right[:, 0:128])
        return jnp.concatenate([left[:, 0:128], middle, right[:, 128:256]], axis=1).astype(BF)

    def attend_row(k):
        row = lax.rem(x + k, SIDE)

        def one(i, carry):
            at = row * TILES_W + i
            att[k, pl.ds(pl.multiple_of(i * 64, 64), 64), :] = pack(attend_tile(at), attend_tile(at + 3))
            return carry

        lax.fori_loop(0, 3, one, 0)

    def mixed_piece(ra, rb, d):
        return gat.at[ra, rb, pl.ds(d * 96, 96), :]

    def start_y(ra):
        for k in range(2):
            for i, (d, step) in enumerate(WAYS):
                d = d ^ k
                src = att.at[0, pl.ds(d * 96, 96), :] if ra == 0 else mixed_piece(ra, 0, d)
                rb = 3 if step == 1 else 1
                ship(src, mixed_piece(ra, rb, d), ysend.at[ra, 2 * k + i], yrecv.at[ra, rb, d], at_xy(0, step))

    def got_y(ra, rb, d):
        wait_recv(mixed_piece(ra, rb, d), ysend.at[0, 0], yrecv.at[ra, rb, d])

    def relay_y(ra):
        for i, (d, step) in enumerate(WAYS):
            rb = 3 if step == 1 else 1
            got_y(ra, rb, d)
            ship(mixed_piece(ra, rb, d), mixed_piece(ra, 2, d), ysend.at[ra, 4 + i], yrecv.at[ra, 2, d],
                 at_xy(0, step))

    def rest_y(ra):
        got_y(ra, 3, 1)
        got_y(ra, 1, 0)
        got_y(ra, 2, 0)
        got_y(ra, 2, 1)

    def add_source(ra, rb, rows, first=False):
        h = lax.rem(x + ra, SIDE) * SIDE + lax.rem(y + rb, SIDE)
        for xi in range(4):
            top = jnp.dot(rows[:, 0:192], wos[xi, h, 64:256, :], preferred_element_type=F32)
            low = jnp.dot(rows[:, 128:384], wos[xi, h, :, :], preferred_element_type=F32)
            if first:
                acc[xi, 0:192, :] = top
                acc[xi, 192:384, :] = low
            else:
                acc[xi, 0:192, :] += top
                acc[xi, 192:384, :] += low

    def add_row(ra, first):
        def one(rb, carry):
            add_source(ra, rb, gat[ra, rb])
            return carry

        lax.fori_loop(first, 4, one, 0)

    def start_x(k):
        ship(att.at[k], gat.at[4 - k, 0], asend.at[k], arecv.at[4 - k], at_xy(k, 0))

    def got_x(ra):
        wait_recv(gat.at[ra, 0], asend.at[0], arecv.at[ra])

    attend_row(0)
    start_y(0)
    attend_row(1)
    start_x(1)
    attend_row(3)
    start_x(3)
    relay_y(0)
    attend_row(2)
    start_x(2)
    wout_rest()
    drain()
    got_x(3)
    start_y(3)
    got_x(1)
    start_y(1)
    got_x(2)
    start_y(2)
    relay_y(3)
    relay_y(1)
    wout_finish()
    add_source(0, 0, att[0], True)
    rest_y(0)
    add_row(0, 1)
    relay_y(2)
    rest_y(3)
    add_row(3, 0)
    rest_y(1)
    add_row(1, 0)
    drain()
    rest_y(2)
    add_row(2, 0)
    def result(xs):
        return out_ref.at[:, pl.ds(pl.multiple_of(xs * 384, 128), 384)]

    for xi in (2, 1, 3):
        outs[xi] = acc[xi].T[0:192].astype(BF)
        ship(outs.at[xi], result(x), osend.at[xi], orecv.at[4 - xi], at_xy(xi, 0))
    out_ref[:, pl.ds(pl.multiple_of(x * 384, 128), 384)] = acc[0].T[0:192].astype(BF)
    for ra in (3, 1, 2):
        wait_recv(result(lax.rem(x + ra, SIDE)), osend.at[0], orecv.at[ra])
    drain()


def on_device(tokens, w_query, w_key, w_value, w_out, q_gain, k_gain, key_tiles, key_count):
    vmem = pl.BlockSpec(memory_space=pltpu.VMEM)
    anywhere = pl.BlockSpec(memory_space=pl.ANY)
    sems = pltpu.SemaphoreType.DMA
    return pl.pallas_call(
        block_kernel,
        out_shape=jax.ShapeDtypeStruct((192, SLOTS), BF),
        in_specs=[anywhere] * 2 + [vmem] * 7,
        out_specs=vmem,
        scratch_shapes=[
            pltpu.SMEM((KT, TILES), jnp.int32),
            pltpu.SMEM((TILES,), jnp.int32),
            pltpu.VMEM((4, 2, 3, HALF, D), BF),
            pltpu.VMEM((4, 2, HALF, D), BF),
            pltpu.VMEM((DEPTH, 192, 768), BF),
            pltpu.VMEM((SLOTS, 256), BF),
            pltpu.VMEM((288, 16, 384), BF),
            pltpu.VMEM((4, DEPTH, 256, 256), BF),
            pltpu.VMEM((4, 8, 192, 128), BF),
            pltpu.VMEM((4, 192, 384), BF),
            pltpu.VMEM((4, 4, 192, 384), BF),
            pltpu.VMEM((4, 384, 256), F32),
            pltpu.VMEM((4, 192, 384), BF),
            sems((2,)),
            sems((2, 5, 6)), sems((2, 4, 4, 2)),
            sems((STREAMS, 2, 8)), sems((STREAMS, 2, 8)),
            sems((STREAMS, 2, 8)), sems((STREAMS, 2, 8)),
            sems((2, 4, 4, 2)), sems((2, 4, 4, 2)),
            sems((4, 6)), sems((4, 6)),
            sems((4, 6)), sems((4, 6)),
            sems((4,)), sems((4,)),
            sems((4, 6)), sems((4, 4, 2)),
            sems((4,)), sems((4,)),
        ],
        compiler_params=pltpu.CompilerParams(
            collective_id=0, has_side_effects=True, vmem_limit_bytes=56 * 1024 * 1024
        ),
        name="block_attention",
    )(key_tiles.T, key_count, tokens, w_query, w_key, w_value, w_out, q_gain[None, :], k_gain[None, :]).T


def solution(mesh):
    in_specs = (
        P(("guidance", "context", "head"), None),
        P("context", "head"),
        P("context", "head"),
        P("context", "head"),
        P("context", "head"),
        P(),
        P(),
        P("context", None),
        P("context"),
    )
    out_specs = P(("guidance", "context"), "head")
    return jax.shard_map(
        on_device, mesh=mesh, in_specs=in_specs, out_specs=out_specs, check_vma=False
    )
```

```python
import jax
import jax.numpy as jnp
from jax import lax
from jax.experimental import pallas as pl
from jax.experimental.pallas import tpu as pltpu
from jax.sharding import PartitionSpec as P

HEAD_DIM = 64
FRAME_H = 30
FRAME_W = 45
TILES_W = 6
TILES = 24
SLOTS = 1536
KT = 8
SIDE = 4
DEPTH = 16
D = 3072
MESH = pl.DeviceIdType.MESH
BF = jnp.bfloat16
F32 = jnp.float32


def place():
    g = lax.axis_index("guidance")
    z = lax.axis_index("context")
    h = lax.axis_index("head")
    return g, z, lax.div(h, SIDE), lax.rem(h, SIDE)


def at_xy(dx, dy):
    g, z, x, y = place()
    return (g, z, lax.rem(x + dx + SIDE, SIDE) * SIDE + lax.rem(y + dy + SIDE, SIDE))


def at_z(dz):
    g, z, x, y = place()
    return (g, lax.rem(z + dz + DEPTH, DEPTH), x * SIDE + y)


def sibling():
    g, z, x, y = place()
    return (1 - g, z, x * SIDE + y)


def send(src, dst, ssem, rsem, device):
    pltpu.make_async_remote_copy(
        src_ref=src, dst_ref=dst, send_sem=ssem, recv_sem=rsem, device_id=device, device_id_type=MESH
    ).start()


def wait_recv(dst, ssem, rsem):
    pltpu.make_async_remote_copy(
        src_ref=dst, dst_ref=dst, send_sem=ssem, recv_sem=rsem, device_id=sibling(), device_id_type=MESH
    ).wait_recv()


def wait_send(src, ssem, rsem):
    pltpu.make_async_remote_copy(
        src_ref=src, dst_ref=src, send_sem=ssem, recv_sem=rsem, device_id=sibling(), device_id_type=MESH
    ).wait_send()


def greet(partners):
    barrier = pltpu.get_barrier_semaphore()
    for partner in partners:
        pl.semaphore_signal(barrier, inc=1, device_id=partner, device_id_type=MESH)
    pl.semaphore_wait(barrier, len(partners))


def head_norm(raw, gain):
    lane_a = lax.broadcasted_iota(jnp.int32, (256, 256), 0) // HEAD_DIM
    lane_b = lax.broadcasted_iota(jnp.int32, (256, 256), 1) // HEAD_DIM
    pick = jnp.where(lane_a == lane_b, 1.0 / HEAD_DIM, 0.0).astype(BF)

    def mean(values):
        high = values.astype(BF)
        low = (values - high.astype(F32)).astype(BF)
        return jnp.dot(high, pick, preferred_element_type=F32) + jnp.dot(
            low, pick, preferred_element_type=F32
        )

    centred = raw - mean(raw)
    spread = mean(centred * centred)
    return centred * lax.rsqrt(spread + 1e-06) * gain


HALF = 48
COLS = D // 2
WAYS = ((0, 1), (1, -1))
STREAMS = 6
ORDER = (0, 3, 1, 2)
SLOT = {0: 0, 3: 1, 1: 2}


def block_kernel(
    tiles_hbm, count_hbm, tok_ref, wq_ref, wk_ref, wv_ref, wo_ref, qg_ref, kg_ref,
    out_ref,
    tiles_ref, count_ref, close, distant, wall, query_ref, kv, wos, pairs, att, gat, acc, outs,
    csem, tsend, trecv, zsend, zrecv, ssend, srecv, hsend, hrecv,
    wsend, wrecv, vsend, vrecv, asend, arecv, ysend, yrecv, osend, orecv,
):
    g, z, x, y = place()
    lists = pltpu.make_async_copy(tiles_hbm, tiles_ref, csem.at[0])
    counts = pltpu.make_async_copy(count_hbm, count_ref, csem.at[1])
    lists.start()
    counts.start()
    greet([
        at_xy(1, 0), at_xy(-1, 0), at_xy(2, 0), at_xy(0, 1), at_xy(0, -1), at_z(1), at_z(-1), sibling()
    ])
    sent = []

    def ship(src, dst, ssem, rsem, device):
        send(src, dst, ssem, rsem, device)
        sent.append((src, ssem, rsem))

    def drain():
        for src, ssem, rsem in sent:
            wait_send(src, ssem, rsem)
        sent.clear()

    def axis_dev(p, second, step):
        along_x = (p == 0) != second
        return at_xy(step, 0) if along_x else at_xy(0, step)

    def piece(p, ra, rb, d):
        at = ORDER.index(ra)
        here = distant.at[at, p] if rb == 2 else close.at[at, p, SLOT[rb]]
        return here.at[:, pl.ds(d * COLS, COLS)]

    def landing(p, rnd, rel, d):
        return piece(p, rel, 0, d) if rnd == 4 else piece(p, rnd, rel, d)

    def own(p, d):
        return tok_ref.at[pl.ds(p * HALF, HALF), pl.ds(d * COLS, COLS)]

    def arrival(p, rnd, rel, d):
        return trecv.at[p, rel, 0, d] if rnd == 4 else trecv.at[p, rnd, rel, d]

    def start(rnd, k):
        for p in range(2):
            for i, (d, step) in enumerate(WAYS):
                d = d ^ k
                src = own(p, d) if rnd in (0, 4) else piece(p, rnd, 0, d)
                rel = 3 if step == 1 else 1
                ship(src, landing(p, rnd, rel, d), tsend.at[p, rnd, 2 * k + i], arrival(p, rnd, rel, d),
                     axis_dev(p, rnd != 4, step))

    def got(p, rnd, rel, d):
        wait_recv(landing(p, rnd, rel, d), tsend.at[p, 0, 0], arrival(p, rnd, rel, d))

    def relay(rnd):
        for p in range(2):
            for i, (d, step) in enumerate(WAYS):
                rel = 3 if step == 1 else 1
                got(p, rnd, rel, d)
                ship(landing(p, rnd, rel, d), landing(p, rnd, 2, d), tsend.at[p, rnd, 4 + i],
                     arrival(p, rnd, 2, d), axis_dev(p, rnd != 4, step))

    def near_rest(rnd):
        for p in range(2):
            got(p, rnd, 3, 1)
            got(p, rnd, 1, 0)

    def far(rnd):
        for p in range(2):
            got(p, rnd, 2, 0)
            got(p, rnd, 2, 1)

    def block(stream, dz, half):
        at = lax.rem(z + dz + DEPTH, DEPTH)
        rows = pl.ds(pl.multiple_of(half * 96 + stream % 2 * 48, 16), 48)
        return wall.at[at, rows, pl.ds(stream // 2 * 256, 256)]

    def steps(stream, way):
        return 8 if (stream + way) % 2 == 0 else 7

    def ship_weights(stream, way, s):
        dz = -s if way == 0 else s
        ship(block(stream, dz, g), block(stream, dz, g), zsend.at[stream, way, s], zrecv.at[stream, way, s],
             at_z(1 if way == 0 else -1))

    def ship_stream(stream):
        for way in range(2):
            ship_weights(stream, way, 0)

    def weight_round(s):
        for stream in range(STREAMS):
            for way in range(2):
                if s > steps(stream, way):
                    continue
                dz = -s if way == 0 else s
                here = block(stream, dz, g)
                wait_recv(here, zsend.at[stream, way, 0], zrecv.at[stream, way, s - 1])
                if s < steps(stream, way):
                    ship_weights(stream, way, s)
                ship(here, here, ssend.at[stream, way, s - 1], srecv.at[stream, way, s - 1], sibling())

    def weights_shared():
        for stream in range(STREAMS):
            for way in range(2):
                for s in range(1, steps(stream, way) + 1):
                    dz = -s if way == 0 else s
                    wait_recv(block(stream, dz, 1 - g), ssend.at[stream, way, 0], srecv.at[stream, way, s - 1])

    start(4, 0)
    wall[z, :, 0:384] = jnp.concatenate([wv_ref[...], wk_ref[...]], axis=1)
    ship_stream(0)
    ship_stream(1)
    start(4, 1)
    wall[z, :, 384:768] = jnp.concatenate([wo_ref[...], wq_ref[...]], axis=1)
    ship_stream(2)
    ship_stream(3)
    for p in range(2):
        close[0, p, 0] = tok_ref[pl.ds(p * HALF, HALF), :]
    wos[:, :, 0:64, :] = jnp.zeros((4, DEPTH, 64, 256), BF)
    ship_stream(4)
    ship_stream(5)

    lane = lax.broadcasted_iota(jnp.int32, (1, 256), 1)
    q_gain = jnp.concatenate([qg_ref[...]] * 4, axis=1) * 0.125
    k_gain = jnp.concatenate([kg_ref[...]] * 4, axis=1)

    def unit(p, ra, rb):
        a_x, a_y = (ra, rb) if p == 0 else (rb, ra)
        return lax.rem(x + a_x, SIDE) * 24 + lax.rem(y + a_y, SIDE) * 6 + p * 3

    def group(rows, pieces):
        raw = jnp.dot(rows, wall[:, :, 0:384].reshape(D, 384), preferred_element_type=F32)
        raw_q = jnp.dot(rows, wall[:, :, 512:768].reshape(D, 256), preferred_element_type=F32)
        raw_k = raw[:, 128:384]
        key = jnp.where(lane >= HEAD_DIM, head_norm(raw_k, k_gain), raw_k)
        query = jnp.where(lane >= HEAD_DIM, head_norm(raw_q, q_gain), 0.0).astype(BF)
        keyval = jnp.concatenate([raw[:, 0:128], key], axis=1).astype(BF)
        for i, (p, ra, rb) in enumerate(pieces):
            at = unit(p, ra, rb)
            part = slice(i * HALF, (i + 1) * HALF)
            query_ref[pl.ds(pl.multiple_of(at * 16, 16), HALF), :] = query[part]
            kv[pl.ds(96 + at, 3)] = keyval[part].reshape(3, 16, 384)
            for way in range(2):
                ship(kv.at[pl.ds(96 + at, 3)], kv.at[pl.ds(192 * way + at, 3)],
                     hsend.at[p, ra, rb, way], hrecv.at[p, ra, rb, way], at_z(1 - 2 * way))

    def near_group(ra):
        group(close[ORDER.index(ra)].reshape(6 * HALF, D), [(p, ra, rb) for p in range(2) for rb in SLOT])

    def far_group(first, last):
        group(distant[first:last].reshape((last - first) * 2 * HALF, D),
              [(p, ORDER[at], 2) for at in range(first, last) for p in range(2)])

    def halo(ra):
        for p in range(2):
            for rb in range(4):
                at = unit(p, ra, rb)
                for way in range(2):
                    wait_recv(kv.at[pl.ds(192 * way + at, 3)], hsend.at[0, 0, 0, 0], hrecv.at[p, ra, rb, way])

    def wout(ra, c, half):
        if c < 4:
            rows = pl.ds(pl.multiple_of(64 + half * 96, 32), 96)
            return wos.at[ra, pl.ds(c * 4, 4), rows, pl.ds(0, 128)]
        return pairs.at[ra, pl.ds((c - 4) * 4, 4), pl.ds(pl.multiple_of(half * 96, 32), 96), :]

    def swap(block):
        return pltpu.roll(block.astype(F32).reshape(8 * 192, 128), 64, 1).reshape(8, 192, 128).astype(BF)

    def wout_own():
        wos[0, :, 64:256, :] = wall[:, :, 384:640]
        lower = lane[:, 0:128].reshape(1, 1, 128) < 64
        pairs[0] = jnp.where(lower, wall[0:8, :, 512:640], swap(wall[8:16, :, 512:640]))

    def wout_start(k):
        for c in range(6):
            step, ra = ((1, 3), (-1, 1))[(c in (2, 3, 5)) ^ k]
            ship(wout(0, c, g), wout(ra, c, g), wsend.at[ra, c], wrecv.at[ra, c], at_xy(step, 0))

    def wout_pass(ra, c):
        wait_recv(wout(ra, c, g), wsend.at[0, 0], wrecv.at[ra, c])
        ship(wout(ra, c, g), wout(ra, c, g), vsend.at[ra, c], vrecv.at[ra, c], sibling())

    def wout_relay():
        for c in range(6):
            step, ra = ((1, 3), (-1, 1))[c in (2, 3, 5)]
            wout_pass(ra, c)
            ship(wout(ra, c, g), wout(2, c, g), wsend.at[2, c], wrecv.at[2, c], at_xy(step, 0))

    def wout_rest():
        for c in range(6):
            wout_pass(1 if c in (0, 1, 4) else 3, c)
        for c in range(6):
            wout_pass(2, c)

    def wout_finish():
        for ra in range(1, 4):
            for c in range(6):
                wait_recv(wout(ra, c, 1 - g), vsend.at[0, 0], vrecv.at[ra, c])
            wos[ra, 0:8, 64:256, 128:256] = pairs[ra]
            wos[ra, 8:16, 64:256, 128:256] = swap(pairs[ra])

    weight_round(1)
    start(0, 0)
    relay(4)
    start(0, 1)
    weight_round(2)
    near_rest(4)
    start(3, 0)
    weight_round(3)
    weight_round(4)
    relay(0)
    start(3, 1)
    start(1, 0)
    weight_round(5)
    weight_round(6)
    relay(3)
    start(1, 1)
    far(4)
    start(2, 0)
    weight_round(7)
    weight_round(8)
    weights_shared()
    near_rest(0)
    near_group(0)
    relay(1)
    start(2, 1)
    near_rest(3)
    near_group(3)
    near_rest(1)
    near_group(1)
    relay(2)
    wout_own()
    wout_start(0)
    far(0)
    far(3)
    far(1)
    far_group(0, 3)
    near_rest(2)
    near_group(2)
    far(2)
    wout_relay()
    wout_start(1)
    far_group(3, 4)
    for ra in ORDER:
        halo(ra)
    lists.wait()
    counts.wait()

    key_lane = lax.broadcasted_iota(jnp.int32, (1, KT * 64), 1)
    slot = lax.rem(key_lane, 64)
    rank = lax.div(key_lane, 64)
    low_row = lax.div(slot, 8) < FRAME_H - 24
    low_col = lax.rem(slot, 8) < FRAME_W - 40
    row_slot = lax.broadcasted_iota(jnp.int32, (64, 1), 0)

    def attend_tile(tile):
        queries = query_ref[pl.ds(pl.multiple_of(tile * 64, 64), 64), :]
        stacked = jnp.concatenate(
            [jnp.where(lax.div(lane, 64) == h + 1, queries, jnp.zeros_like(queries)) for h in range(3)], axis=0
        )
        count = count_ref[tile]
        near = []
        row_last = jnp.zeros_like(key_lane)
        col_last = jnp.zeros_like(key_lane)
        for j in range(KT):
            index = jnp.clip(tiles_ref[j, tile] - (z - 1) * TILES, 0, 3 * TILES - 1)
            near += [kv[4 * index + i] for i in range(4)]
            within = lax.rem(index, TILES)
            here = rank == j
            row_last = jnp.where(here, (within >= 18).astype(jnp.int32), row_last)
            col_last = jnp.where(here, (lax.rem(within, TILES_W) == TILES_W - 1).astype(jnp.int32), col_last)
        near = jnp.concatenate(near, axis=0)
        keep = (rank < count) & ((row_last == 0) | low_row) & ((col_last == 0) | low_col)
        scores = lax.dot_general(
            stacked, near[:, 128:384], (((1,), (1,)), ((), ())), preferred_element_type=F32
        )
        scores = jnp.where(keep, scores, -1e30)
        top = jnp.max(scores, axis=-1, keepdims=True)
        weights = jnp.exp(scores - top).astype(BF)
        values = jnp.where(lane >= 192, jnp.ones((), BF), near[:, 0:256])
        mixed = jnp.dot(weights, values, preferred_element_type=F32)
        mixed = mixed / mixed[:, 192:193]
        result = jnp.where(
            lane < 64, mixed[0:64], jnp.where(lane < 128, mixed[64:128], mixed[128:192])
        )
        row, col = lax.div(tile, TILES_W), lax.rem(tile, TILES_W)
        alive = (row * 8 + lax.div(row_slot, 8) < FRAME_H) & (col * 8 + lax.rem(row_slot, 8) < FRAME_W)
        return jnp.where(alive, result, 0.0)

    def pack(left, right):
        right = pltpu.roll(right, 64, 1)
        middle = jnp.where(lane[:, 0:128] < 64, left[:, 128:256], right[:, 0:128])
        return jnp.concatenate([left[:, 0:128], middle, right[:, 128:256]], axis=1).astype(BF)

    def attend_row(k):
        row = lax.rem(x + k, SIDE)

        def one(i, carry):
            at = row * TILES_W + i
            att[k, pl.ds(pl.multiple_of(i * 64, 64), 64), :] = pack(attend_tile(at), attend_tile(at + 3))
            return carry

        lax.fori_loop(0, 3, one, 0)

    def mixed_piece(ra, rb, d):
        return gat.at[ra, rb, pl.ds(d * 96, 96), :]

    def start_y(ra):
        for k in range(2):
            for i, (d, step) in enumerate(WAYS):
                d = d ^ k
                src = att.at[0, pl.ds(d * 96, 96), :] if ra == 0 else mixed_piece(ra, 0, d)
                rb = 3 if step == 1 else 1
                ship(src, mixed_piece(ra, rb, d), ysend.at[ra, 2 * k + i], yrecv.at[ra, rb, d], at_xy(0, step))

    def got_y(ra, rb, d):
        wait_recv(mixed_piece(ra, rb, d), ysend.at[0, 0], yrecv.at[ra, rb, d])

    def relay_y(ra):
        for i, (d, step) in enumerate(WAYS):
            rb = 3 if step == 1 else 1
            got_y(ra, rb, d)
            ship(mixed_piece(ra, rb, d), mixed_piece(ra, 2, d), ysend.at[ra, 4 + i], yrecv.at[ra, 2, d],
                 at_xy(0, step))

    def rest_y(ra):
        got_y(ra, 3, 1)
        got_y(ra, 1, 0)
        got_y(ra, 2, 0)
        got_y(ra, 2, 1)

    def add_source(ra, rb, rows, first=False, targets=range(4)):
        h = lax.rem(x + ra, SIDE) * SIDE + lax.rem(y + rb, SIDE)
        for xi in targets:
            top = jnp.dot(rows[:, 0:192], wos[xi, h, 64:256, :], preferred_element_type=F32)
            low = jnp.dot(rows[:, 128:384], wos[xi, h, :, :], preferred_element_type=F32)
            if first:
                acc[xi, 0:192, :] = top
                acc[xi, 192:384, :] = low
            else:
                acc[xi, 0:192, :] += top
                acc[xi, 192:384, :] += low

    def add_row(ra, first):
        def one(rb, carry):
            add_source(ra, rb, gat[ra, rb])
            return carry

        lax.fori_loop(first, 4, one, 0)

    def start_x(k):
        ship(att.at[k], gat.at[4 - k, 0], asend.at[k], arecv.at[4 - k], at_xy(k, 0))

    def got_x(ra):
        wait_recv(gat.at[ra, 0], asend.at[0], arecv.at[ra])

    attend_row(0)
    start_y(0)
    attend_row(1)
    start_x(1)
    attend_row(3)
    start_x(3)
    relay_y(0)
    attend_row(2)
    start_x(2)
    wout_rest()
    drain()
    got_x(3)
    start_y(3)
    got_x(1)
    start_y(1)
    got_x(2)
    start_y(2)
    relay_y(3)
    relay_y(1)
    wout_finish()
    add_source(0, 0, att[0], True)
    rest_y(0)
    add_row(0, 1)
    relay_y(2)
    rest_y(3)
    add_row(3, 0)
    rest_y(1)
    add_row(1, 0)
    drain()
    rest_y(2)
    def result(xs):
        return out_ref.at[:, pl.ds(pl.multiple_of(xs * 384, 128), 384)]

    def finish(xi):
        def one(rb, carry):
            add_source(2, rb, gat[2, rb], targets=(xi,))
            return carry

        lax.fori_loop(0, 4, one, 0)
        return acc[xi].T[0:192].astype(BF)

    for xi in (2, 1, 3):
        outs[xi] = finish(xi)
        ship(outs.at[xi], result(x), osend.at[xi], orecv.at[4 - xi], at_xy(xi, 0))
    out_ref[:, pl.ds(pl.multiple_of(x * 384, 128), 384)] = finish(0)
    for ra in (3, 1, 2):
        wait_recv(result(lax.rem(x + ra, SIDE)), osend.at[0], orecv.at[ra])
    drain()


def on_device(tokens, w_query, w_key, w_value, w_out, q_gain, k_gain, key_tiles, key_count):
    vmem = pl.BlockSpec(memory_space=pltpu.VMEM)
    anywhere = pl.BlockSpec(memory_space=pl.ANY)
    sems = pltpu.SemaphoreType.DMA
    return pl.pallas_call(
        block_kernel,
        out_shape=jax.ShapeDtypeStruct((192, SLOTS), BF),
        in_specs=[anywhere] * 2 + [vmem] * 7,
        out_specs=vmem,
        scratch_shapes=[
            pltpu.SMEM((KT, TILES), jnp.int32),
            pltpu.SMEM((TILES,), jnp.int32),
            pltpu.VMEM((4, 2, 3, HALF, D), BF),
            pltpu.VMEM((4, 2, HALF, D), BF),
            pltpu.VMEM((DEPTH, 192, 768), BF),
            pltpu.VMEM((SLOTS, 256), BF),
            pltpu.VMEM((288, 16, 384), BF),
            pltpu.VMEM((4, DEPTH, 256, 256), BF),
            pltpu.VMEM((4, 8, 192, 128), BF),
            pltpu.VMEM((4, 192, 384), BF),
            pltpu.VMEM((4, 4, 192, 384), BF),
            pltpu.VMEM((4, 384, 256), F32),
            pltpu.VMEM((4, 192, 384), BF),
            sems((2,)),
            sems((2, 5, 6)), sems((2, 4, 4, 2)),
            sems((STREAMS, 2, 8)), sems((STREAMS, 2, 8)),
            sems((STREAMS, 2, 8)), sems((STREAMS, 2, 8)),
            sems((2, 4, 4, 2)), sems((2, 4, 4, 2)),
            sems((4, 6)), sems((4, 6)),
            sems((4, 6)), sems((4, 6)),
            sems((4,)), sems((4,)),
            sems((4, 6)), sems((4, 4, 2)),
            sems((4,)), sems((4,)),
        ],
        compiler_params=pltpu.CompilerParams(
            collective_id=0, has_side_effects=True, vmem_limit_bytes=56 * 1024 * 1024
        ),
        name="block_attention",
    )(key_tiles.T, key_count, tokens, w_query, w_key, w_value, w_out, q_gain[None, :], k_gain[None, :]).T


def solution(mesh):
    in_specs = (
        P(("guidance", "context", "head"), None),
        P("context", "head"),
        P("context", "head"),
        P("context", "head"),
        P("context", "head"),
        P(),
        P(),
        P("context", None),
        P("context"),
    )
    out_specs = P(("guidance", "context"), "head")
    return jax.shard_map(
        on_device, mesh=mesh, in_specs=in_specs, out_specs=out_specs, check_vma=False
    )
```

```python
import jax
import jax.numpy as jnp
from jax import lax
from jax.experimental import pallas as pl
from jax.experimental.pallas import tpu as pltpu
from jax.sharding import PartitionSpec as P

HEAD_DIM = 64
FRAME_H = 30
FRAME_W = 45
TILES_W = 6
TILES = 24
SLOTS = 1536
KT = 8
SIDE = 4
DEPTH = 16
D = 3072
MESH = pl.DeviceIdType.MESH
BF = jnp.bfloat16
F32 = jnp.float32


def place():
    g = lax.axis_index("guidance")
    z = lax.axis_index("context")
    h = lax.axis_index("head")
    return g, z, lax.div(h, SIDE), lax.rem(h, SIDE)


def at_xy(dx, dy):
    g, z, x, y = place()
    return (g, z, lax.rem(x + dx + SIDE, SIDE) * SIDE + lax.rem(y + dy + SIDE, SIDE))


def at_z(dz):
    g, z, x, y = place()
    return (g, lax.rem(z + dz + DEPTH, DEPTH), x * SIDE + y)


def sibling():
    g, z, x, y = place()
    return (1 - g, z, x * SIDE + y)


def send(src, dst, ssem, rsem, device):
    pltpu.make_async_remote_copy(
        src_ref=src, dst_ref=dst, send_sem=ssem, recv_sem=rsem, device_id=device, device_id_type=MESH
    ).start()


def wait_recv(dst, ssem, rsem):
    pltpu.make_async_remote_copy(
        src_ref=dst, dst_ref=dst, send_sem=ssem, recv_sem=rsem, device_id=sibling(), device_id_type=MESH
    ).wait_recv()


def wait_send(src, ssem, rsem):
    pltpu.make_async_remote_copy(
        src_ref=src, dst_ref=src, send_sem=ssem, recv_sem=rsem, device_id=sibling(), device_id_type=MESH
    ).wait_send()


def greet(partners):
    barrier = pltpu.get_barrier_semaphore()
    for partner in partners:
        pl.semaphore_signal(barrier, inc=1, device_id=partner, device_id_type=MESH)
    pl.semaphore_wait(barrier, len(partners))


def head_norm(raw, gain):
    lane_a = lax.broadcasted_iota(jnp.int32, (256, 256), 0) // HEAD_DIM
    lane_b = lax.broadcasted_iota(jnp.int32, (256, 256), 1) // HEAD_DIM
    pick = jnp.where(lane_a == lane_b, 1.0 / HEAD_DIM, 0.0).astype(BF)

    def mean(values):
        high = values.astype(BF)
        low = (values - high.astype(F32)).astype(BF)
        return jnp.dot(high, pick, preferred_element_type=F32) + jnp.dot(
            low, pick, preferred_element_type=F32
        )

    centred = raw - mean(raw)
    spread = mean(centred * centred)
    return centred * lax.rsqrt(spread + 1e-06) * gain


HALF = 48
COLS = D // 2
WAYS = ((0, 1), (1, -1))
STREAMS = 6
ORDER = (0, 3, 1, 2)
SLOT = {0: 0, 3: 1, 1: 2}


def block_kernel(
    tiles_hbm, count_hbm, tok_ref, wq_ref, wk_ref, wv_ref, wo_ref, qg_ref, kg_ref,
    out_ref,
    tiles_ref, count_ref, close, distant, wall, query_ref, kv, wos, pairs, att, gat, acc, outs,
    csem, tsend, trecv, zsend, zrecv, ssend, srecv, hsend, hrecv,
    wsend, wrecv, vsend, vrecv, asend, arecv, ysend, yrecv, osend, orecv,
):
    g, z, x, y = place()
    lists = pltpu.make_async_copy(tiles_hbm, tiles_ref, csem.at[0])
    counts = pltpu.make_async_copy(count_hbm, count_ref, csem.at[1])
    lists.start()
    counts.start()
    greet([
        at_xy(1, 0), at_xy(-1, 0), at_xy(2, 0), at_xy(0, 1), at_xy(0, -1), at_z(1), at_z(-1), sibling()
    ])
    sent = []

    def ship(src, dst, ssem, rsem, device):
        send(src, dst, ssem, rsem, device)
        sent.append((src, ssem, rsem))

    def drain(count):
        for src, ssem, rsem in sent[:count]:
            wait_send(src, ssem, rsem)
        del sent[:count]

    def axis_dev(p, second, step):
        along_x = (p == 0) != second
        return at_xy(step, 0) if along_x else at_xy(0, step)

    def piece(p, ra, rb, d):
        at = ORDER.index(ra)
        here = distant.at[at, p] if rb == 2 else close.at[at, p, SLOT[rb]]
        return here.at[:, pl.ds(d * COLS, COLS)]

    def landing(p, rnd, rel, d):
        return piece(p, rel, 0, d) if rnd == 4 else piece(p, rnd, rel, d)

    def own(p, d):
        return tok_ref.at[pl.ds(p * HALF, HALF), pl.ds(d * COLS, COLS)]

    def arrival(p, rnd, rel, d):
        return trecv.at[p, rel, 0, d] if rnd == 4 else trecv.at[p, rnd, rel, d]

    def start(rnd, k):
        for p in range(2):
            for i, (d, step) in enumerate(WAYS):
                d = d ^ k
                src = own(p, d) if rnd in (0, 4) else piece(p, rnd, 0, d)
                rel = 3 if step == 1 else 1
                ship(src, landing(p, rnd, rel, d), tsend.at[p, rnd, 2 * k + i], arrival(p, rnd, rel, d),
                     axis_dev(p, rnd != 4, step))

    def got(p, rnd, rel, d):
        wait_recv(landing(p, rnd, rel, d), tsend.at[p, 0, 0], arrival(p, rnd, rel, d))

    def relay(rnd):
        for p in range(2):
            for i, (d, step) in enumerate(WAYS):
                rel = 3 if step == 1 else 1
                got(p, rnd, rel, d)
                ship(landing(p, rnd, rel, d), landing(p, rnd, 2, d), tsend.at[p, rnd, 4 + i],
                     arrival(p, rnd, 2, d), axis_dev(p, rnd != 4, step))

    def near_rest(rnd):
        for p in range(2):
            got(p, rnd, 3, 1)
            got(p, rnd, 1, 0)

    def far(rnd):
        for p in range(2):
            got(p, rnd, 2, 0)
            got(p, rnd, 2, 1)

    def block(stream, dz, half):
        at = lax.rem(z + dz + DEPTH, DEPTH)
        rows = pl.ds(pl.multiple_of(half * 96 + stream % 2 * 48, 16), 48)
        return wall.at[at, rows, pl.ds(stream // 2 * 256, 256)]

    def steps(stream, way):
        return 8 if (stream + way) % 2 == 0 else 7

    def ship_weights(stream, way, s):
        dz = -s if way == 0 else s
        ship(block(stream, dz, g), block(stream, dz, g), zsend.at[stream, way, s], zrecv.at[stream, way, s],
             at_z(1 if way == 0 else -1))

    def ship_stream(stream):
        for way in range(2):
            ship_weights(stream, way, 0)

    def weight_round(s):
        for stream in range(STREAMS):
            for way in range(2):
                if s > steps(stream, way):
                    continue
                dz = -s if way == 0 else s
                here = block(stream, dz, g)
                wait_recv(here, zsend.at[stream, way, 0], zrecv.at[stream, way, s - 1])
                if s < steps(stream, way):
                    ship_weights(stream, way, s)
                ship(here, here, ssend.at[stream, way, s - 1], srecv.at[stream, way, s - 1], sibling())

    def weights_shared():
        for stream in range(STREAMS):
            for way in range(2):
                for s in range(1, steps(stream, way) + 1):
                    dz = -s if way == 0 else s
                    wait_recv(block(stream, dz, 1 - g), ssend.at[stream, way, 0], srecv.at[stream, way, s - 1])

    start(4, 0)
    wall[z, :, 0:384] = jnp.concatenate([wv_ref[...], wk_ref[...]], axis=1)
    ship_stream(0)
    ship_stream(1)
    start(4, 1)
    wall[z, :, 384:768] = jnp.concatenate([wo_ref[...], wq_ref[...]], axis=1)
    ship_stream(2)
    ship_stream(3)
    for p in range(2):
        close[0, p, 0] = tok_ref[pl.ds(p * HALF, HALF), :]
    wos[:, :, 0:64, :] = jnp.zeros((4, DEPTH, 64, 256), BF)
    ship_stream(4)
    ship_stream(5)

    lane = lax.broadcasted_iota(jnp.int32, (1, 256), 1)
    q_gain = jnp.concatenate([qg_ref[...]] * 4, axis=1) * 0.125
    k_gain = jnp.concatenate([kg_ref[...]] * 4, axis=1)

    def unit(p, ra, rb):
        a_x, a_y = (ra, rb) if p == 0 else (rb, ra)
        return lax.rem(x + a_x, SIDE) * 24 + lax.rem(y + a_y, SIDE) * 6 + p * 3

    def group(rows, pieces):
        raw = jnp.dot(rows, wall[:, :, 0:384].reshape(D, 384), preferred_element_type=F32)
        raw_q = jnp.dot(rows, wall[:, :, 512:768].reshape(D, 256), preferred_element_type=F32)
        raw_k = raw[:, 128:384]
        key = jnp.where(lane >= HEAD_DIM, head_norm(raw_k, k_gain), raw_k)
        query = jnp.where(lane >= HEAD_DIM, head_norm(raw_q, q_gain), 0.0).astype(BF)
        keyval = jnp.concatenate([raw[:, 0:128], key], axis=1).astype(BF)
        for i, (p, ra, rb) in enumerate(pieces):
            at = unit(p, ra, rb)
            part = slice(i * HALF, (i + 1) * HALF)
            query_ref[pl.ds(pl.multiple_of(at * 16, 16), HALF), :] = query[part]
            kv[pl.ds(96 + at, 3)] = keyval[part].reshape(3, 16, 384)
            for way in range(2):
                ship(kv.at[pl.ds(96 + at, 3)], kv.at[pl.ds(192 * way + at, 3)],
                     hsend.at[p, ra, rb, way], hrecv.at[p, ra, rb, way], at_z(1 - 2 * way))

    def near_group(ra):
        group(close[ORDER.index(ra)].reshape(6 * HALF, D), [(p, ra, rb) for p in range(2) for rb in SLOT])

    def far_group(first, last):
        group(distant[first:last].reshape((last - first) * 2 * HALF, D),
              [(p, ORDER[at], 2) for at in range(first, last) for p in range(2)])

    def halo(ra):
        for p in range(2):
            for rb in range(4):
                at = unit(p, ra, rb)
                for way in range(2):
                    wait_recv(kv.at[pl.ds(192 * way + at, 3)], hsend.at[0, 0, 0, 0], hrecv.at[p, ra, rb, way])

    def wout(ra, c, half):
        if c < 4:
            rows = pl.ds(pl.multiple_of(64 + half * 96, 32), 96)
            return wos.at[ra, pl.ds(c * 4, 4), rows, pl.ds(0, 128)]
        return pairs.at[ra, pl.ds((c - 4) * 4, 4), pl.ds(pl.multiple_of(half * 96, 32), 96), :]

    def swap(block):
        return pltpu.roll(block.astype(F32).reshape(8 * 192, 128), 64, 1).reshape(8, 192, 128).astype(BF)

    def wout_own():
        wos[0, :, 64:256, :] = wall[:, :, 384:640]
        lower = lane[:, 0:128].reshape(1, 1, 128) < 64
        pairs[0] = jnp.where(lower, wall[0:8, :, 512:640], swap(wall[8:16, :, 512:640]))

    def wout_start(k):
        for c in range(6):
            step, ra = ((1, 3), (-1, 1))[(c in (2, 3, 5)) ^ k]
            ship(wout(0, c, g), wout(ra, c, g), wsend.at[ra, c], wrecv.at[ra, c], at_xy(step, 0))

    def wout_pass(ra, c):
        wait_recv(wout(ra, c, g), wsend.at[0, 0], wrecv.at[ra, c])
        ship(wout(ra, c, g), wout(ra, c, g), vsend.at[ra, c], vrecv.at[ra, c], sibling())

    def wout_relay():
        for c in range(6):
            step, ra = ((1, 3), (-1, 1))[c in (2, 3, 5)]
            wout_pass(ra, c)
            ship(wout(ra, c, g), wout(2, c, g), wsend.at[2, c], wrecv.at[2, c], at_xy(step, 0))

    def wout_rest():
        for c in range(6):
            wout_pass(1 if c in (0, 1, 4) else 3, c)
        for c in range(6):
            wout_pass(2, c)

    def wout_finish():
        for ra in range(1, 4):
            for c in range(6):
                wait_recv(wout(ra, c, 1 - g), vsend.at[0, 0], vrecv.at[ra, c])
            wos[ra, 0:8, 64:256, 128:256] = pairs[ra]
            wos[ra, 8:16, 64:256, 128:256] = swap(pairs[ra])

    weight_round(1)
    start(0, 0)
    relay(4)
    start(0, 1)
    weight_round(2)
    near_rest(4)
    start(3, 0)
    weight_round(3)
    weight_round(4)
    relay(0)
    start(3, 1)
    start(1, 0)
    weight_round(5)
    weight_round(6)
    relay(3)
    start(1, 1)
    far(4)
    start(2, 0)
    weight_round(7)
    weight_round(8)
    weights_shared()
    near_rest(0)
    near_group(0)
    relay(1)
    start(2, 1)
    near_rest(3)
    near_group(3)
    near_rest(1)
    near_group(1)
    relay(2)
    projected = len(sent)
    wout_own()
    wout_start(0)
    far(0)
    far(3)
    far(1)
    far_group(0, 3)
    near_rest(2)
    near_group(2)
    far(2)
    wout_relay()
    wout_start(1)
    far_group(3, 4)
    drain(projected)
    for ra in ORDER:
        halo(ra)
    shared = len(sent)
    lists.wait()
    counts.wait()

    key_lane = lax.broadcasted_iota(jnp.int32, (1, KT * 64), 1)
    slot = lax.rem(key_lane, 64)
    rank = lax.div(key_lane, 64)
    low_row = lax.div(slot, 8) < FRAME_H - 24
    low_col = lax.rem(slot, 8) < FRAME_W - 40
    row_slot = lax.broadcasted_iota(jnp.int32, (64, 1), 0)

    def attend_tile(tile):
        queries = query_ref[pl.ds(pl.multiple_of(tile * 64, 64), 64), :]
        stacked = jnp.concatenate(
            [jnp.where(lax.div(lane, 64) == h + 1, queries, jnp.zeros_like(queries)) for h in range(3)], axis=0
        )
        count = count_ref[tile]
        near = []
        row_last = jnp.zeros_like(key_lane)
        col_last = jnp.zeros_like(key_lane)
        for j in range(KT):
            index = jnp.clip(tiles_ref[j, tile] - (z - 1) * TILES, 0, 3 * TILES - 1)
            near += [kv[4 * index + i] for i in range(4)]
            within = lax.rem(index, TILES)
            here = rank == j
            row_last = jnp.where(here, (within >= 18).astype(jnp.int32), row_last)
            col_last = jnp.where(here, (lax.rem(within, TILES_W) == TILES_W - 1).astype(jnp.int32), col_last)
        near = jnp.concatenate(near, axis=0)
        keep = (rank < count) & ((row_last == 0) | low_row) & ((col_last == 0) | low_col)
        scores = lax.dot_general(
            stacked, near[:, 128:384], (((1,), (1,)), ((), ())), preferred_element_type=F32
        )
        scores = jnp.where(keep, scores, -1e30)
        top = jnp.max(scores, axis=-1, keepdims=True)
        weights = jnp.exp(scores - top).astype(BF)
        values = jnp.where(lane >= 192, jnp.ones((), BF), near[:, 0:256])
        mixed = jnp.dot(weights, values, preferred_element_type=F32)
        mixed = mixed * (1.0 / mixed[:, 192:193])
        result = jnp.where(
            lane < 64, mixed[0:64], jnp.where(lane < 128, mixed[64:128], mixed[128:192])
        )
        row, col = lax.div(tile, TILES_W), lax.rem(tile, TILES_W)
        alive = (row * 8 + lax.div(row_slot, 8) < FRAME_H) & (col * 8 + lax.rem(row_slot, 8) < FRAME_W)
        return jnp.where(alive, result, 0.0)

    def pack(left, right):
        right = pltpu.roll(right, 64, 1)
        middle = jnp.where(lane[:, 0:128] < 64, left[:, 128:256], right[:, 0:128])
        return jnp.concatenate([left[:, 0:128], middle, right[:, 128:256]], axis=1).astype(BF)

    def attend_row(k):
        row = lax.rem(x + k, SIDE)

        def one(i, carry):
            at = row * TILES_W + i
            att[k, pl.ds(pl.multiple_of(i * 64, 64), 64), :] = pack(attend_tile(at), attend_tile(at + 3))
            return carry

        lax.fori_loop(0, 3, one, 0)

    def mixed_piece(ra, rb, d):
        return gat.at[ra, rb, pl.ds(d * 96, 96), :]

    def start_y(ra):
        for k in range(2):
            for i, (d, step) in enumerate(WAYS):
                d = d ^ k
                src = att.at[0, pl.ds(d * 96, 96), :] if ra == 0 else mixed_piece(ra, 0, d)
                rb = 3 if step == 1 else 1
                ship(src, mixed_piece(ra, rb, d), ysend.at[ra, 2 * k + i], yrecv.at[ra, rb, d], at_xy(0, step))

    def got_y(ra, rb, d):
        wait_recv(mixed_piece(ra, rb, d), ysend.at[0, 0], yrecv.at[ra, rb, d])

    def relay_y(ra):
        for i, (d, step) in enumerate(WAYS):
            rb = 3 if step == 1 else 1
            got_y(ra, rb, d)
            ship(mixed_piece(ra, rb, d), mixed_piece(ra, 2, d), ysend.at[ra, 4 + i], yrecv.at[ra, 2, d],
                 at_xy(0, step))

    def rest_y(ra):
        got_y(ra, 3, 1)
        got_y(ra, 1, 0)
        got_y(ra, 2, 0)
        got_y(ra, 2, 1)

    def add_source(ra, rb, rows, first=False, targets=range(4)):
        h = lax.rem(x + ra, SIDE) * SIDE + lax.rem(y + rb, SIDE)
        for xi in targets:
            top = jnp.dot(rows[:, 0:192], wos[xi, h, 64:256, :], preferred_element_type=F32)
            low = jnp.dot(rows[:, 128:384], wos[xi, h, :, :], preferred_element_type=F32)
            if first:
                acc[xi, 0:192, :] = top
                acc[xi, 192:384, :] = low
            else:
                acc[xi, 0:192, :] += top
                acc[xi, 192:384, :] += low

    def add_row(ra, first):
        def one(rb, carry):
            add_source(ra, rb, gat[ra, rb])
            return carry

        lax.fori_loop(first, 4, one, 0)

    def start_x(k):
        ship(att.at[k], gat.at[4 - k, 0], asend.at[k], arecv.at[4 - k], at_xy(k, 0))

    def got_x(ra):
        wait_recv(gat.at[ra, 0], asend.at[0], arecv.at[ra])

    attend_row(0)
    start_y(0)
    attend_row(1)
    start_x(1)
    attend_row(3)
    start_x(3)
    relay_y(0)
    attend_row(2)
    start_x(2)
    wout_rest()
    got_x(3)
    start_y(3)
    got_x(1)
    start_y(1)
    got_x(2)
    start_y(2)
    drain(shared)
    relay_y(3)
    relay_y(1)
    wout_finish()
    add_source(0, 0, att[0], True)
    rest_y(0)
    add_row(0, 1)
    relay_y(2)
    rest_y(3)
    add_row(3, 0)
    rest_y(1)
    add_row(1, 0)
    drain(len(sent))
    rest_y(2)
    def result(xs):
        return out_ref.at[:, pl.ds(pl.multiple_of(xs * 384, 128), 384)]

    def finish(xi):
        def one(rb, carry):
            add_source(2, rb, gat[2, rb], targets=(xi,))
            return carry

        lax.fori_loop(0, 4, one, 0)
        return acc[xi].T[0:192].astype(BF)

    for xi in (2, 1, 3):
        outs[xi] = finish(xi)
        ship(outs.at[xi], result(x), osend.at[xi], orecv.at[4 - xi], at_xy(xi, 0))
    out_ref[:, pl.ds(pl.multiple_of(x * 384, 128), 384)] = finish(0)
    for ra in (3, 1, 2):
        wait_recv(result(lax.rem(x + ra, SIDE)), osend.at[0], orecv.at[ra])
    drain(len(sent))


def on_device(tokens, w_query, w_key, w_value, w_out, q_gain, k_gain, key_tiles, key_count):
    vmem = pl.BlockSpec(memory_space=pltpu.VMEM)
    anywhere = pl.BlockSpec(memory_space=pl.ANY)
    sems = pltpu.SemaphoreType.DMA
    return pl.pallas_call(
        block_kernel,
        out_shape=jax.ShapeDtypeStruct((192, SLOTS), BF),
        in_specs=[anywhere] * 2 + [vmem] * 7,
        out_specs=vmem,
        scratch_shapes=[
            pltpu.SMEM((KT, TILES), jnp.int32),
            pltpu.SMEM((TILES,), jnp.int32),
            pltpu.VMEM((4, 2, 3, HALF, D), BF),
            pltpu.VMEM((4, 2, HALF, D), BF),
            pltpu.VMEM((DEPTH, 192, 768), BF),
            pltpu.VMEM((SLOTS, 256), BF),
            pltpu.VMEM((288, 16, 384), BF),
            pltpu.VMEM((4, DEPTH, 256, 256), BF),
            pltpu.VMEM((4, 8, 192, 128), BF),
            pltpu.VMEM((4, 192, 384), BF),
            pltpu.VMEM((4, 4, 192, 384), BF),
            pltpu.VMEM((4, 384, 256), F32),
            pltpu.VMEM((4, 192, 384), BF),
            sems((2,)),
            sems((2, 5, 6)), sems((2, 4, 4, 2)),
            sems((STREAMS, 2, 8)), sems((STREAMS, 2, 8)),
            sems((STREAMS, 2, 8)), sems((STREAMS, 2, 8)),
            sems((2, 4, 4, 2)), sems((2, 4, 4, 2)),
            sems((4, 6)), sems((4, 6)),
            sems((4, 6)), sems((4, 6)),
            sems((4,)), sems((4,)),
            sems((4, 6)), sems((4, 4, 2)),
            sems((4,)), sems((4,)),
        ],
        compiler_params=pltpu.CompilerParams(
            collective_id=0, has_side_effects=True, vmem_limit_bytes=56 * 1024 * 1024
        ),
        name="block_attention",
    )(key_tiles.T, key_count, tokens, w_query, w_key, w_value, w_out, q_gain[None, :], k_gain[None, :]).T


def solution(mesh):
    in_specs = (
        P(("guidance", "context", "head"), None),
        P("context", "head"),
        P("context", "head"),
        P("context", "head"),
        P("context", "head"),
        P(),
        P(),
        P("context", None),
        P("context"),
    )
    out_specs = P(("guidance", "context"), "head")
    return jax.shard_map(
        on_device, mesh=mesh, in_specs=in_specs, out_specs=out_specs, check_vma=False
    )
```
